32 devices in a mesh: sample: 4 (over y, x), space: 8 (over z, core).
Axes of the slice: x: 2, y: 2, z: 4, core: 2. Of those that a mesh axis runs over, the one named last changes fastest.
Arguments:
- slabs: bfloat16 [4, 64, 32, 3072], P('sample', 'space'), may hold values from -6 to 6
- weight: bfloat16 [3, 3, 3, 96, 192], replicated, may hold values from -0.125 to 0.125
- cotangent: bfloat16 [4, 32, 16, 3072], P('sample', 'space'), may hold values from -6 to 6
Outputs:
- activation: bfloat16 [4, 32, 16, 3072], P('sample', 'space')
- input_grad: bfloat16 [4, 64, 32, 3072], P('sample', 'space')
- weight_grad: float32 [3, 3, 3, 96, 192], P(None, None, None, None, 'space')
The draws below stay inside these ranges and needn't reach their ends.
All inputs are finite; a program needn't handle non-finite values.
Results may differ from the reference program's by a relative error of at most 0.007.
Values may be sent and summed in bfloat16 or wider, within the bound.
No kernel may reach another device: no remote copies, remote signals or barrier semaphores. Data moves between devices by JAX's collectives and lax.ppermute only.
A program may use at most 64 MiB of HBM per device.

```python
import jax
import jax.numpy as jnp
from jax import lax

CIN = 96
COUT = 192
DEPTH = 64
H = 32
W = 32
BATCH = 4
DOUT = 32
HOUT = 16
WOUT = 16


def spiked(array, own_key, source, target, blocks, factor):
    owner, partner = [(jnp.arange(array.shape[axis_at]) // (array.shape[axis_at] // blocks)).reshape([-1 if axis == axis_at else 1 for axis in range(array.ndim)]) for axis_at in (source, target)]
    chosen = jax.random.permutation(own_key, blocks)[partner]
    strong = (owner == chosen) | (owner == (partner + blocks // 2) % blocks)
    return jnp.where(strong, factor * array, array)


def block_scale(own_key, dims, split, smallest, high):
    def one(position, shards_of):
        draws = jax.random.uniform(jax.random.fold_in(jax.random.fold_in(own_key, 6), position), (shards_of,), jnp.float32, smallest / len(split), high / len(split))
        return jnp.repeat(jnp.exp(draws), dims[position] // shards_of).reshape((-1,) + (1,) * (len(dims) - position - 1))

    gain = one(*split[0])
    for cut in split[1:]:
        gain = gain * one(*cut)
    return gain


def normal_values(stream_key, dims, width, limit, cuts=(), dtype=jnp.bfloat16):
    entries = jax.random.normal(stream_key, dims, jnp.float32) * width
    if len(cuts) > 0:
        entries = block_scale(stream_key, dims, cuts, -0.22, 0.18) * entries
    return jnp.clip(entries, min=-limit, max=limit).astype(dtype)


def gaussian_with(stream_key, dims, spread, bound, cuts, heavy, held_as=jnp.bfloat16):
    values = spread * jax.random.normal(stream_key, dims, jnp.float32)
    if cuts:
        values = values * block_scale(stream_key, dims, cuts, -0.22, 0.18)
    return jnp.clip(spiked(values, jax.random.fold_in(stream_key, 3), *heavy), -bound, bound).astype(held_as)


def setup_inputs(seed: int = 0) -> dict:
    seeds = jax.random.split(jax.random.key(seed), 4)
    slabs = normal_values(seeds[0], (BATCH, DEPTH, H, W * CIN), 1.0, 6.0, ((0, 4), (1, 8)))
    weight = normal_values(seeds[1], (3, 3, 3, CIN, COUT), (27 * CIN) ** -0.5, 0.125)
    cotangent = gaussian_with(seeds[2], (BATCH, DOUT, HOUT, WOUT * COUT), 1.0, 6.0, ((0, 4), (1, 8)), (0, 1, 4, 2.0))
    return {"slabs": slabs, "weight": weight, "cotangent": cotangent}


layout_names = ('NDHWC', 'DHWIO', 'NDHWC')

def conv_forward(field, weight, margins):
    return lax.conv_general_dilated(field.astype(jnp.float32), weight.astype(jnp.float32), (2, 2, 2), margins, dimension_numbers=layout_names, precision=lax.Precision.HIGHEST)

def conv_input_grad(grad_pre, weight, extents, margins):
    flipped = jnp.transpose(weight[::-1, ::-1, ::-1], (0, 1, 2, 4, 3)).astype(jnp.float32)
    padding = []
    for extent, margin in zip(extents, margins):
        remain = (extent + margin[0] + margin[1] - 3) % 2
        padding.append((2 - margin[0], 2 - margin[1] + remain))
    return lax.conv_general_dilated(grad_pre.astype(jnp.float32), flipped, (1, 1, 1), padding, lhs_dilation=(2, 2, 2), dimension_numbers=layout_names, precision=lax.Precision.HIGHEST)

def weight_grad(field, grad_pre, margins):
    padded = jnp.pad(field, ((0, 0), margins[0], margins[1], margins[2], (0, 0))).astype(jnp.float32)
    grad_wide = grad_pre.astype(jnp.float32)
    out_d, out_h, out_w = (grad_pre.shape[1], grad_pre.shape[2], grad_pre.shape[3])
    collected = []
    for depth_off in range(3):
        for row_off in range(3):
            for col_off in range(3):
                window = padded[:, depth_off:depth_off + 2 * out_d - 1:2, row_off:row_off + 2 * out_h - 1:2, col_off:col_off + 2 * out_w - 1:2]
                collected.append(jnp.einsum('ndhwc,ndhwo->co', window, grad_wide, precision=lax.Precision.HIGHEST))
    return jnp.stack(collected).reshape(3, 3, 3, field.shape[-1], grad_pre.shape[-1])

def derivative(preact):
    sigmoid_val = jax.nn.sigmoid(preact)
    return sigmoid_val * (1.0 + preact * (1.0 - sigmoid_val))

def reference(slabs, weight, cotangent):
    margins = ((1, 1), (1, 1), (1, 1))

    def one_sample(running, sample_pair):
        sample_cells, sample_cot = sample_pair
        field = sample_cells.reshape(1, DEPTH, H, W, CIN)
        preact = conv_forward(field, weight, margins)
        result = jax.nn.silu(preact).astype(jnp.bfloat16)
        grad_pre = (sample_cot.reshape(preact.shape).astype(jnp.float32) * derivative(preact)).astype(jnp.bfloat16)
        grad_in = conv_input_grad(grad_pre, weight, (DEPTH, H, W), margins).astype(jnp.bfloat16)
        running = running + weight_grad(field, grad_pre, margins)
        return (running, (result.reshape(DOUT, HOUT, WOUT * COUT), grad_in.reshape(DEPTH, H, W * CIN)))
    start = jnp.zeros((3, 3, 3, CIN, COUT), jnp.float32)
    running, (activation, input_grad) = lax.scan(one_sample, start, (slabs, cotangent))
    return (activation, input_grad, running / BATCH)
```

```python
import functools

import jax
import jax.numpy as jnp
from jax import lax
from jax.experimental import pallas as pl
from jax.experimental.pallas import tpu as pltpu
from jax.sharding import PartitionSpec as P

CIN = 96
COUT = 192
BLOCK = 384
SPAN = 512
TAPS = 9
TERM_TILES = -(-TAPS * 3 * CIN // 128)
F32 = jnp.float32
BF16 = jnp.bfloat16
VMEM_LIMIT = 12 * 1024 * 1024


def iota(shape, axis):
    return lax.broadcasted_iota(jnp.int32, shape, axis)


def row_split(planes):
    shape = (3 * planes * 16, planes * 32)
    row = iota(shape, 0)
    col = iota(shape, 1)
    j = row & 15
    plane = (row >> 4) & (planes - 1)
    b = jnp.where(row >= planes * 32, 2, jnp.where(row >= planes * 16, 1, 0))
    hit = (col == plane * 32 + 2 * j + b - 1) & ((j + b) > 0)
    return jnp.where(hit, 1.0, 0.0).astype(BF16)


def blank(rows, lanes):
    return jnp.zeros((rows, lanes), BF16)


def dot(lhs, rhs):
    return jnp.dot(lhs, rhs, preferred_element_type=F32)


def dot_nt(lhs, rhs):
    return lax.dot_general(lhs, rhs, (((1,), (1,)), ((), ())), preferred_element_type=F32)


def put(wide, per_out, cells, i, m, tap, piece):
    at = i * per_out + m * 16
    wide[at : at + 16, tap * SPAN + 128 : tap * SPAN + 512] = piece
    if m + 1 < cells:
        wide[at + 16 : at + 32, tap * SPAN : tap * SPAN + 128] = piece[:, 256:]
    if m == 0:
        wide[at : at + 16, tap * SPAN : tap * SPAN + 128] = jnp.zeros((16, 128), BF16)


def edge_kernel(x_hbm, edge_ref, sem):
    copy = pltpu.make_async_copy(x_hbm.at[x_hbm.shape[0] - 1], edge_ref, sem)
    copy.start()
    copy.wait()


def own_kernel(
    planes, x_hbm, w_hbm, cot_hbm, wide, band, preact, cot_ref, x_ref, w_ref, sems
):
    outs = planes // 2
    cells = x_ref.shape[2] // BLOCK
    per_out = cells * 16
    x_copy = pltpu.make_async_copy(x_hbm, x_ref, sems.at[0])
    w_copy = pltpu.make_async_copy(w_hbm, w_ref, sems.at[1])
    cot_copy = pltpu.make_async_copy(cot_hbm, cot_ref, sems.at[2])
    x_copy.start()
    w_copy.start()
    cot_copy.start()
    split = row_split(planes)
    wide[0:per_out, 0 : 3 * SPAN] = jnp.zeros((per_out, 3 * SPAN), BF16)
    x_copy.wait()
    x = x_ref[...].reshape(planes * 32, x_ref.shape[2])
    for m in range(cells):
        rows = dot(split, x[:, m * BLOCK : (m + 1) * BLOCK]).astype(BF16)
        for b in range(3):
            for p in range(planes):
                piece = rows[(b * planes + p) * 16 : (b * planes + p + 1) * 16]
                if p % 2 == 0:
                    put(wide, per_out, cells, p // 2, m, 3 + b, piece)
                else:
                    put(wide, per_out, cells, p // 2, m, 6 + b, piece)
                    if p // 2 + 1 < outs:
                        put(wide, per_out, cells, p // 2 + 1, m, b, piece)
    w_copy.wait()
    for tap in range(TAPS):
        w = w_ref[tap]
        even = jnp.concatenate([blank(32, COUT), w, blank(192, COUT)], axis=0)
        odd = jnp.concatenate([blank(224, COUT), w], axis=0)
        band[tap * SPAN : (tap + 1) * SPAN] = jnp.concatenate([even, odd], axis=1)
    preact[...] = dot(wide[...], band[...])
    cot_copy.wait()


def add_terms(turned, edge, wide, terms):
    rows = terms.shape[0]
    per_out = edge.shape[0]
    terms[...] = jnp.zeros_like(terms)
    lane = iota((rows, SPAN), 1)
    even_lanes = (lane >= 32) & (lane < 320)
    odd_lanes = lane >= 224
    for tap in range(TAPS):
        lanes = slice(tap * SPAN, (tap + 1) * SPAN)
        if tap < 3:
            cols = jnp.concatenate([edge[:, lanes], wide[per_out:, lanes]], axis=0)
        else:
            cols = wide[:, lanes]
        both = dot(turned, cols)
        base = tap * 288 // 128 * 128
        shift = tap * 288 - base
        even = jnp.where(even_lanes, both[:rows], 0.0)
        odd = jnp.where(odd_lanes, both[rows:], 0.0)
        even = pltpu.roll(even, (shift - 32) % SPAN, 1)
        odd = pltpu.roll(odd, (shift - 224) % SPAN, 1)
        terms[:, base : base + BLOCK] += (even + odd)[:, :BLOCK]


def share(terms, send_ref, keep_ref):
    rows = send_ref.shape[0]
    send_ref[...] = terms[:rows].astype(BF16)
    keep_ref[...] = terms[rows:]


def halo_kernel(
    width, above_ref, wide, band, pre_ref, cot_ref,
    act_ref, gp_ref, first_ref, turned_ref, edge, send_ref, keep_ref, terms,
):
    outs = cot_ref.shape[0]
    cells = cot_ref.shape[2] // BLOCK
    per_out = cells * 16
    at = lax.axis_index("space")
    core = at % 2
    chip = at // 2
    split_one = row_split(1)
    for m in range(cells):
        lanes = slice(m * BLOCK, (m + 1) * BLOCK)
        plane = above_ref[:, lanes]
        plane = jnp.where(core + chip == 0, jnp.zeros_like(plane), plane)
        above = dot(split_one, plane).astype(BF16)
        for b in range(3):
            put(edge, per_out, cells, 0, m, b, above[b * 16 : b * 16 + 16])
    added = dot(edge[...], band[: 3 * SPAN])
    for i in range(outs):
        for m in range(cells):
            lanes = slice(m * BLOCK, (m + 1) * BLOCK)
            at = i * per_out + m * 16
            value = pre_ref[at : at + 16]
            if i == 0:
                value = value + added[at : at + 16]
            sig = jax.nn.sigmoid(value)
            act_ref[i, :, lanes] = (value * sig).astype(BF16)
            grad = cot_ref[i, :, lanes].astype(F32) * (sig * (1.0 + value * (1.0 - sig)))
            grad = grad.astype(BF16)
            gp_ref[at : at + 16] = grad
            if i == 0:
                first_ref[at : at + 16] = grad

    rows = send_ref.shape[0]
    half = lax.axis_size("space") // 4
    high = rows // half
    shape = (8 * rows, 2 * COUT)
    inner = iota(shape, 0)
    later = inner >= 4 * rows
    inner = inner - jnp.where(later, 4 * rows, 0)
    odd = inner >= 2 * rows
    inner = inner - jnp.where(odd, 2 * rows, 0)
    kept = inner >= rows
    inner = inner - jnp.where(kept, rows, 0)
    source = jnp.where(kept, core, 1 - core) * width + jnp.where(odd, COUT, 0)
    for k in range(half):
        channel = inner - k * high
        inside = (channel >= 0) & (channel < width)
        target = jnp.where(later, chip ^ k, chip ^ (k + half)) * 2 * width
        source = source + jnp.where(inside, channel + target, 0)
        if high != width:
            source = jnp.where((channel >= width) & (channel < high), -1, source)
    order = jnp.where(iota(shape, 1) == source, 1.0, 0.0).astype(BF16)
    turned_ref[...] = dot_nt(order, gp_ref[...]).astype(BF16)
    add_terms(turned_ref[: 4 * rows], edge, wide, terms)
    share(terms, send_ref, keep_ref)


def later_kernel(turned_ref, edge, wide, send_ref, keep_ref, terms):
    add_terms(turned_ref[4 * send_ref.shape[0] :], edge, wide, terms)
    share(terms, send_ref, keep_ref)


def input_kernel(gp_ref, below_ref, band, out_ref):
    per_out = below_ref.shape[0]
    cells = per_out // 16
    here = gp_ref[...]
    following = below_ref[...]
    last = lax.axis_index("space") == lax.axis_size("space") - 1
    following = jnp.where(last, jnp.zeros_like(following), following)
    there = jnp.concatenate([here[per_out:], following], axis=0)
    count = gp_ref.shape[0]
    outs = count // per_out
    shape = (128, 128)
    row = iota(shape, 0)
    below = jnp.where((iota(shape, 1) == row + 1) & ((row & 15) != 15), 1.0, 0.0).astype(BF16)

    def lowered(block):
        return jnp.concatenate(
            [dot(below, block[at : at + 128]).astype(BF16) for at in range(0, count, 128)], axis=0
        )

    here_low = lowered(here)
    there_low = lowered(there)

    def term(grad, a, b):
        tap = a * 3 + b
        return dot_nt(grad, band[tap * SPAN : (tap + 1) * SPAN])

    groups = {
        (0, 0): term(here, 1, 1),
        (0, 1): term(here, 1, 2) + term(here_low, 1, 0),
        (1, 0): term(here, 2, 1) + term(there, 0, 1),
        (1, 1): term(here, 2, 2) + term(here_low, 2, 0) + term(there, 0, 2) + term(there_low, 0, 0),
    }
    shape = (32, 32)
    row = iota(shape, 0)
    weave = jnp.where(iota(shape, 1) == (row >> 1) + (row & 1) * 16, 1.0, 0.0).astype(BF16)
    for i in range(outs):
        for m in range(cells):
            at = i * per_out + m * 16
            for pd in range(2):
                parts = []
                for ph in range(2):
                    y = groups[pd, ph]
                    body = y[at : at + 16, 128:512]
                    if m + 1 < cells:
                        body = jnp.concatenate(
                            [body[:, :256], body[:, 256:] + y[at + 16 : at + 32, :128]], axis=1
                        )
                    parts.append(body.astype(BF16))
                mixed = dot(weave, jnp.concatenate(parts, axis=0)).astype(BF16)
                out_ref[2 * i + pd, :, m * BLOCK : (m + 1) * BLOCK] = mixed


def early_pair_kernel(keep_ref, got_ref, *out_refs):
    total = keep_ref[...] + got_ref[...].astype(F32)
    high = out_refs[0].shape[0]
    for k, ref in enumerate(out_refs):
        ref[...] = total[k * high : (k + 1) * high].astype(ref.dtype)


def later_pair_kernel(early_ref, keep_ref, got_ref, first_ref, passed_ref, *out_refs):
    del early_ref
    passed_ref[...] = first_ref[...]
    early_pair_kernel(keep_ref, got_ref, *out_refs)


def depth_kernel(own_ref, *refs):
    total = own_ref[...]
    for ref in refs[:-1]:
        total = total + ref[...].astype(F32)
    refs[-1][...] = total.astype(BF16)


def sample_kernel(scale, *refs):
    out_ref = refs[-1]
    parts = [ref[...].astype(F32) for ref in refs[:-1]]
    while len(parts) > 1:
        parts = [parts[n] + parts[n + 1] for n in range(0, len(parts), 2)]
    total = parts[0][: out_ref.shape[1]] * scale
    for n in range(out_ref.shape[0]):
        out_ref[n] = total[:, n * CIN : (n + 1) * CIN]


def flipped(size, bits):
    return [(i, i ^ bits) for i in range(size)]


def per_device(slabs, weight, cotangent):
    samples, planes, rows, lanes = slabs.shape
    outs = planes // 2
    space = lax.axis_size("space")
    sample = lax.axis_size("sample")
    depth = space // 2
    width = COUT // space
    high = -(-width // 8) * 8
    half = depth // 2
    part = (high, TERM_TILES * 128)
    group = (half * high, TERM_TILES * 128)
    cells = lanes // BLOCK
    per_out = cells * 16
    count = outs * per_out

    in_chip = flipped(space, 1)
    onward = [(i, (i + 1) % space) for i in range(space)]
    back = [(b, a) for a, b in onward]

    x = slabs.reshape(planes, rows, lanes)
    cot = cotangent.reshape(outs, rows // 2, lanes)
    w = weight.reshape(TAPS, 3 * CIN, COUT)
    x, cot, w = (pltpu.with_memory_space_constraint(array, pltpu.HBM) for array in (x, cot, w))
    vmem = pl.BlockSpec(memory_space=pltpu.VMEM)
    hbm = pl.BlockSpec(memory_space=pltpu.HBM)
    params = pltpu.CompilerParams(vmem_limit_bytes=VMEM_LIMIT)
    shape = jax.ShapeDtypeStruct
    flops = 2 * count * TAPS * SPAN * BLOCK

    edge = pl.pallas_call(
        edge_kernel,
        out_shape=shape((rows, lanes), BF16),
        in_specs=[hbm],
        out_specs=vmem,
        scratch_shapes=[pltpu.SemaphoreType.DMA(())],
        compiler_params=params,
        name="edge_plane",
    )(x)
    above = lax.ppermute(edge, "space", onward)
    wide, band, preact, cot_in = pl.pallas_call(
        functools.partial(own_kernel, planes),
        out_shape=(
            shape((count, TAPS * SPAN), BF16),
            shape((TAPS * SPAN, BLOCK), BF16),
            shape((count, BLOCK), F32),
            shape(cot.shape, BF16),
        ),
        in_specs=[hbm] * 3,
        out_specs=(vmem,) * 4,
        scratch_shapes=[
            pltpu.VMEM(x.shape, BF16),
            pltpu.VMEM(w.shape, BF16),
            pltpu.SemaphoreType.DMA((3,)),
        ],
        compiler_params=params,
        cost_estimate=pl.CostEstimate(flops=flops, bytes_accessed=12 << 20, transcendentals=0),
        name="own_planes",
    )(x, w, cot)

    terms = pltpu.VMEM((2 * group[0], group[1]), F32)
    act, grad, first, turned, halo, send, keep = pl.pallas_call(
        functools.partial(halo_kernel, width),
        out_shape=(
            shape(cot.shape, BF16),
            shape((count, BLOCK), BF16),
            shape((per_out, BLOCK), BF16),
            shape((8 * group[0], count), BF16),
            shape((per_out, 3 * SPAN), BF16),
            shape(group, BF16),
            shape(group, F32),
        ),
        in_specs=[vmem] * 5,
        out_specs=(vmem,) * 7,
        scratch_shapes=[terms],
        compiler_params=params,
        cost_estimate=pl.CostEstimate(
            flops=flops // 2, bytes_accessed=8 << 20, transcendentals=count * BLOCK
        ),
        name="halo_and_early_half",
    )(above, wide, band, preact, cot_in)
    got = lax.ppermute(send, "space", in_chip)
    later_send, later_keep = pl.pallas_call(
        later_kernel,
        out_shape=(shape(group, BF16), shape(group, F32)),
        in_specs=[vmem] * 3,
        out_specs=(vmem,) * 2,
        scratch_shapes=[terms],
        compiler_params=params,
        cost_estimate=pl.CostEstimate(flops=flops // 2, bytes_accessed=8 << 20, transcendentals=0),
        name="later_half",
    )(turned, halo, wide)
    later_got = lax.ppermute(later_send, "space", in_chip)

    early = pl.pallas_call(
        early_pair_kernel,
        out_shape=(shape(part, BF16),) * half,
        in_specs=[vmem] * 2,
        out_specs=(vmem,) * half,
        compiler_params=params,
        name="early_pair_sum",
    )(keep, got)
    came = [
        lax.ppermute(early[k - half], "space", flipped(space, 2 * k))
        for k in reversed(range(half, depth))
    ]
    first, own, *later = pl.pallas_call(
        later_pair_kernel,
        out_shape=(shape(first.shape, BF16), shape(part, F32)) + (shape(part, BF16),) * (half - 1),
        in_specs=[vmem] * 4,
        out_specs=(vmem,) * (half + 1),
        compiler_params=params,
        name="later_pair_sum",
    )(early[0], later_keep, later_got, first)
    came += [lax.ppermute(later[k - 1], "space", flipped(space, 2 * k)) for k in range(1, half)]
    below = lax.ppermute(first, "space", back)

    grad_in = pl.pallas_call(
        input_kernel,
        out_shape=shape(x.shape, BF16),
        in_specs=[vmem] * 3,
        out_specs=vmem,
        compiler_params=params,
        cost_estimate=pl.CostEstimate(flops=flops, bytes_accessed=8 << 20, transcendentals=0),
        name="input_grad",
    )(grad, below, band)

    total = pl.pallas_call(
        depth_kernel,
        out_shape=shape(part, BF16),
        in_specs=[vmem] * depth,
        out_specs=vmem,
        compiler_params=params,
        name="depth_sum",
    )(own, *came)
    others = [lax.ppermute(total, "sample", flipped(sample, j)) for j in range(1, sample)]
    kernel_grad = pl.pallas_call(
        functools.partial(sample_kernel, 1.0 / (samples * sample)),
        out_shape=shape((TAPS * 3, width, CIN), F32),
        in_specs=[vmem] * sample,
        out_specs=vmem,
        compiler_params=params,
        name="sample_sum",
    )(total, *others)
    kernel_grad = jnp.transpose(kernel_grad, (0, 2, 1)).reshape(3, 3, 3, CIN, width)
    return act.reshape(cotangent.shape), grad_in.reshape(slabs.shape), kernel_grad


def solution(mesh):
    placed = (P("sample", "space", None, None), P(), P("sample", "space", None, None))
    return jax.shard_map(
        per_device,
        mesh=mesh,
        in_specs=placed,
        out_specs=(
            P("sample", "space", None, None),
            P("sample", "space", None, None),
            P(None, None, None, None, "space"),
        ),
        check_vma=False,
    )
```

```python
import functools

import jax
import jax.numpy as jnp
from jax import lax
from jax.experimental import pallas as pl
from jax.experimental.pallas import tpu as pltpu
from jax.sharding import PartitionSpec as P

CIN = 96
COUT = 192
BLOCK = 384
SPAN = 512
TAPS = 9
LOW = 640
HIGH = 768
MINE = LOW + HIGH
F32 = jnp.float32
BF16 = jnp.bfloat16
VMEM_LIMIT = 12 * 1024 * 1024


def iota(shape, axis):
    return lax.broadcasted_iota(jnp.int32, shape, axis)


def row_split(planes):
    shape = (3 * planes * 16, planes * 32)
    row = iota(shape, 0)
    col = iota(shape, 1)
    j = row & 15
    plane = (row >> 4) & (planes - 1)
    b = jnp.where(row >= planes * 32, 2, jnp.where(row >= planes * 16, 1, 0))
    hit = (col == plane * 32 + 2 * j + b - 1) & ((j + b) > 0)
    return jnp.where(hit, 1.0, 0.0).astype(BF16)


def blank(rows, lanes):
    return jnp.zeros((rows, lanes), BF16)


def dot(lhs, rhs):
    return jnp.dot(lhs, rhs, preferred_element_type=F32)


def dot_nt(lhs, rhs):
    return lax.dot_general(lhs, rhs, (((1,), (1,)), ((), ())), preferred_element_type=F32)


def put(wide, per_out, cells, i, m, tap, piece):
    at = i * per_out + m * 16
    wide[at : at + 16, tap * SPAN + 128 : tap * SPAN + 512] = piece
    if m + 1 < cells:
        wide[at + 16 : at + 32, tap * SPAN : tap * SPAN + 128] = piece[:, 256:]
    if m == 0:
        wide[at : at + 16, tap * SPAN : tap * SPAN + 128] = jnp.zeros((16, 128), BF16)


def edge_kernel(x_hbm, edge_ref, sem):
    copy = pltpu.make_async_copy(x_hbm.at[x_hbm.shape[0] - 1], edge_ref, sem)
    copy.start()
    copy.wait()


def own_kernel(
    planes, x_hbm, w_hbm, cot_hbm, wide, band, preact, cot_ref, x_ref, w_ref, sems
):
    outs = planes // 2
    cells = x_ref.shape[2] // BLOCK
    per_out = cells * 16
    x_copy = pltpu.make_async_copy(x_hbm, x_ref, sems.at[0])
    w_copy = pltpu.make_async_copy(w_hbm, w_ref, sems.at[1])
    cot_copy = pltpu.make_async_copy(cot_hbm, cot_ref, sems.at[2])
    x_copy.start()
    w_copy.start()
    cot_copy.start()
    split = row_split(planes)
    wide[0:per_out, 0 : 3 * SPAN] = jnp.zeros((per_out, 3 * SPAN), BF16)
    x_copy.wait()
    x = x_ref[...].reshape(planes * 32, x_ref.shape[2])
    for m in range(cells):
        rows = dot(split, x[:, m * BLOCK : (m + 1) * BLOCK]).astype(BF16)
        for b in range(3):
            for p in range(planes):
                piece = rows[(b * planes + p) * 16 : (b * planes + p + 1) * 16]
                if p % 2 == 0:
                    put(wide, per_out, cells, p // 2, m, 3 + b, piece)
                else:
                    put(wide, per_out, cells, p // 2, m, 6 + b, piece)
                    if p // 2 + 1 < outs:
                        put(wide, per_out, cells, p // 2 + 1, m, b, piece)
    w_copy.wait()
    for tap in range(TAPS):
        w = w_ref[tap]
        even = jnp.concatenate([blank(32, COUT), w, blank(192, COUT)], axis=0)
        odd = jnp.concatenate([blank(224, COUT), w], axis=0)
        band[tap * SPAN : (tap + 1) * SPAN] = jnp.concatenate([even, odd], axis=1)
    preact[...] = dot(wide[...], band[...])
    cot_copy.wait()


def add_terms(turned, edge, wide, terms):
    rows = terms.shape[0]
    per_out = edge.shape[0]
    terms[...] = jnp.zeros_like(terms)
    lane = iota((rows, SPAN), 1)
    even_lanes = (lane >= 32) & (lane < 320)
    odd_lanes = lane >= 224
    for tap in range(TAPS):
        lanes = slice(tap * SPAN, (tap + 1) * SPAN)
        if tap < 3:
            cols = jnp.concatenate([edge[:, lanes], wide[per_out:, lanes]], axis=0)
        else:
            cols = wide[:, lanes]
        both = dot(turned, cols)
        base = tap * 288 // 128 * 128
        shift = tap * 288 - base
        even = jnp.where(even_lanes, both[:rows], 0.0)
        odd = jnp.where(odd_lanes, both[rows:], 0.0)
        even = pltpu.roll(even, (shift - 32) % SPAN, 1)
        odd = pltpu.roll(odd, (shift - 224) % SPAN, 1)
        terms[:, base : base + BLOCK] += (even + odd)[:, :BLOCK]


def halo_kernel(
    width, above_ref, wide, band, pre_ref, cot_ref,
    act_ref, gp_ref, first_ref, turned_ref, edge, send_ref, terms,
):
    outs = cot_ref.shape[0]
    cells = cot_ref.shape[2] // BLOCK
    per_out = cells * 16
    at = lax.axis_index("space")
    core = at % 2
    chip = at // 2
    split_one = row_split(1)
    for m in range(cells):
        lanes = slice(m * BLOCK, (m + 1) * BLOCK)
        plane = above_ref[:, lanes]
        plane = jnp.where(core + chip == 0, jnp.zeros_like(plane), plane)
        above = dot(split_one, plane).astype(BF16)
        for b in range(3):
            put(edge, per_out, cells, 0, m, b, above[b * 16 : b * 16 + 16])
    added = dot(edge[...], band[: 3 * SPAN])
    for i in range(outs):
        for m in range(cells):
            lanes = slice(m * BLOCK, (m + 1) * BLOCK)
            at = i * per_out + m * 16
            value = pre_ref[at : at + 16]
            if i == 0:
                value = value + added[at : at + 16]
            sig = jax.nn.sigmoid(value)
            act_ref[i, :, lanes] = (value * sig).astype(BF16)
            grad = cot_ref[i, :, lanes].astype(F32) * (sig * (1.0 + value * (1.0 - sig)))
            grad = grad.astype(BF16)
            gp_ref[at : at + 16] = grad
            if i == 0:
                first_ref[at : at + 16] = grad

    rows = send_ref.shape[0]
    steps = lax.axis_size("space") // 2
    high = rows // steps
    shape = (4 * rows, 2 * COUT)
    inner = iota(shape, 0)
    kept = inner >= 2 * rows
    inner = inner - jnp.where(kept, 2 * rows, 0)
    odd = inner >= rows
    inner = inner - jnp.where(odd, rows, 0)
    source = jnp.where(kept, core, 1 - core) * width + jnp.where(odd, COUT, 0)
    for k in range(steps):
        channel = inner - k * high
        inside = (channel >= 0) & (channel < width)
        source = source + jnp.where(inside, channel + (chip ^ k) * 2 * width, 0)
        if high != width:
            source = jnp.where((channel >= width) & (channel < high), -1, source)
    order = jnp.where(iota(shape, 1) == source, 1.0, 0.0).astype(BF16)
    turned_ref[...] = dot_nt(order, gp_ref[...]).astype(BF16)
    add_terms(turned_ref[: 2 * rows], edge, wide, terms)
    send_ref[...] = terms[...].astype(BF16)


def keep_kernel(turned_ref, edge, wide, keep_ref):
    add_terms(turned_ref[2 * keep_ref.shape[0] :], edge, wide, keep_ref)


def input_kernel(gp_ref, below_ref, band, out_ref, done_ref):
    done_ref[...] = jnp.zeros_like(done_ref)
    per_out = below_ref.shape[0]
    cells = per_out // 16
    here = gp_ref[...]
    following = below_ref[...]
    last = lax.axis_index("space") == lax.axis_size("space") - 1
    following = jnp.where(last, jnp.zeros_like(following), following)
    there = jnp.concatenate([here[per_out:], following], axis=0)
    count = gp_ref.shape[0]
    outs = count // per_out
    shape = (128, 128)
    row = iota(shape, 0)
    below = jnp.where((iota(shape, 1) == row + 1) & ((row & 15) != 15), 1.0, 0.0).astype(BF16)

    def lowered(block):
        return jnp.concatenate(
            [dot(below, block[at : at + 128]).astype(BF16) for at in range(0, count, 128)], axis=0
        )

    here_low = lowered(here)
    there_low = lowered(there)

    def term(grad, a, b):
        tap = a * 3 + b
        return dot_nt(grad, band[tap * SPAN : (tap + 1) * SPAN])

    groups = {
        (0, 0): term(here, 1, 1),
        (0, 1): term(here, 1, 2) + term(here_low, 1, 0),
        (1, 0): term(here, 2, 1) + term(there, 0, 1),
        (1, 1): term(here, 2, 2) + term(here_low, 2, 0) + term(there, 0, 2) + term(there_low, 0, 0),
    }
    shape = (32, 32)
    row = iota(shape, 0)
    weave = jnp.where(iota(shape, 1) == (row >> 1) + (row & 1) * 16, 1.0, 0.0).astype(BF16)
    for i in range(outs):
        for m in range(cells):
            at = i * per_out + m * 16
            for pd in range(2):
                parts = []
                for ph in range(2):
                    y = groups[pd, ph]
                    body = y[at : at + 16, 128:512]
                    if m + 1 < cells:
                        body = jnp.concatenate(
                            [body[:, :256], body[:, 256:] + y[at + 16 : at + 32, :128]], axis=1
                        )
                    parts.append(body.astype(BF16))
                mixed = dot(weave, jnp.concatenate(parts, axis=0)).astype(BF16)
                out_ref[2 * i + pd, :, m * BLOCK : (m + 1) * BLOCK] = mixed


def sample_bits():
    at = lax.axis_index("sample")
    return at % 2, at // (lax.axis_size("sample") // 2)


def pair_kernel(keep_ref, got_ref, mine_ref, low_ref, high_ref):
    def total(start, lanes):
        lanes = pl.ds(pl.multiple_of(start, 128), lanes)
        return keep_ref[:, lanes] + got_ref[:, lanes].astype(F32)

    low, high = sample_bits()
    low_ref[...] = total((1 - low) * LOW, LOW).astype(BF16)
    high_ref[...] = total(2 * LOW + (1 - high) * HIGH, HIGH).astype(BF16)
    mine_ref[:, :LOW] = total(low * LOW, LOW)
    mine_ref[:, LOW:] = total(2 * LOW + high * HIGH, HIGH)


def cross_kernel(mine_ref, low_ref, high_ref, *out_refs):
    for lanes, ref in ((slice(0, LOW), low_ref), (slice(LOW, MINE), high_ref)):
        total = mine_ref[:, lanes] + ref[...].astype(F32)
        high = out_refs[0].shape[0]
        for k, out_ref in enumerate(out_refs):
            out_ref[:, lanes] = total[k * high : (k + 1) * high].astype(out_ref.dtype)


def depth_kernel(done_ref, own_ref, *refs):
    del done_ref
    total = own_ref[...]
    for ref in refs[:-1]:
        total = total + ref[...].astype(F32)
    refs[-1][...] = total.astype(BF16)


def tree(parts):
    while len(parts) > 1:
        parts = [parts[n] + parts[n + 1] for n in range(0, len(parts), 2)]
    return parts[0]


def sample_kernel(scale, *refs):
    out_ref = refs[-1]
    width = out_ref.shape[1]
    parts = [ref[...].astype(F32)[:width] * scale for ref in refs[:-1]]
    half = len(parts) // 2
    here = tree([part[:, :LOW] for part in parts[0::2]])
    there = tree([part[:, :LOW] for part in parts[1::2]])
    above = tree([part[:, LOW:] for part in parts[:half]])
    below = tree([part[:, LOW:] for part in parts[half:]])
    low, high = (bit == 0 for bit in sample_bits())
    total = jnp.concatenate(
        [
            jnp.where(low, here, there),
            jnp.where(low, there, here),
            jnp.where(high, above, below),
            jnp.where(high, below, above),
        ],
        axis=1,
    )
    for n in range(out_ref.shape[0]):
        out_ref[n] = total[:, n * CIN : (n + 1) * CIN]


def flipped(size, bits):
    return [(i, i ^ bits) for i in range(size)]


def per_device(slabs, weight, cotangent):
    samples, planes, rows, lanes = slabs.shape
    outs = planes // 2
    space = lax.axis_size("space")
    sample = lax.axis_size("sample")
    depth = space // 2
    width = COUT // space
    high = -(-width // 8) * 8
    kept_rows = depth * high
    terms = (kept_rows, 2 * MINE)
    part = (high, MINE)
    cells = lanes // BLOCK
    per_out = cells * 16
    count = outs * per_out

    in_chip = flipped(space, 1)
    onward = [(i, (i + 1) % space) for i in range(space)]
    back = [(b, a) for a, b in onward]

    x = slabs.reshape(planes, rows, lanes)
    cot = cotangent.reshape(outs, rows // 2, lanes)
    w = weight.reshape(TAPS, 3 * CIN, COUT)
    x, cot, w = (pltpu.with_memory_space_constraint(array, pltpu.HBM) for array in (x, cot, w))
    vmem = pl.BlockSpec(memory_space=pltpu.VMEM)
    hbm = pl.BlockSpec(memory_space=pltpu.HBM)
    params = pltpu.CompilerParams(vmem_limit_bytes=VMEM_LIMIT)
    shape = jax.ShapeDtypeStruct
    flops = 2 * count * TAPS * SPAN * BLOCK

    edge = pl.pallas_call(
        edge_kernel,
        out_shape=shape((rows, lanes), BF16),
        in_specs=[hbm],
        out_specs=vmem,
        scratch_shapes=[pltpu.SemaphoreType.DMA(())],
        compiler_params=params,
        name="edge_plane",
    )(x)
    above = lax.ppermute(edge, "space", onward)
    wide, band, preact, cot_in = pl.pallas_call(
        functools.partial(own_kernel, planes),
        out_shape=(
            shape((count, TAPS * SPAN), BF16),
            shape((TAPS * SPAN, BLOCK), BF16),
            shape((count, BLOCK), F32),
            shape(cot.shape, BF16),
        ),
        in_specs=[hbm] * 3,
        out_specs=(vmem,) * 4,
        scratch_shapes=[
            pltpu.VMEM(x.shape, BF16),
            pltpu.VMEM(w.shape, BF16),
            pltpu.SemaphoreType.DMA((3,)),
        ],
        compiler_params=params,
        cost_estimate=pl.CostEstimate(flops=flops, bytes_accessed=12 << 20, transcendentals=0),
        name="own_planes",
    )(x, w, cot)

    act, grad, first, turned, halo, send = pl.pallas_call(
        functools.partial(halo_kernel, width),
        out_shape=(
            shape(cot.shape, BF16),
            shape((count, BLOCK), BF16),
            shape((per_out, BLOCK), BF16),
            shape((4 * kept_rows, count), BF16),
            shape((per_out, 3 * SPAN), BF16),
            shape(terms, BF16),
        ),
        in_specs=[vmem] * 5,
        out_specs=(vmem,) * 6,
        scratch_shapes=[pltpu.VMEM(terms, F32)],
        compiler_params=params,
        cost_estimate=pl.CostEstimate(
            flops=flops // 2, bytes_accessed=8 << 20, transcendentals=count * BLOCK
        ),
        name="halo_and_sent_half",
    )(above, wide, band, preact, cot_in)
    got = lax.ppermute(send, "space", in_chip)
    below = lax.ppermute(first, "space", back)
    keep = pl.pallas_call(
        keep_kernel,
        out_shape=shape(terms, F32),
        in_specs=[vmem] * 3,
        out_specs=vmem,
        compiler_params=params,
        cost_estimate=pl.CostEstimate(flops=flops // 2, bytes_accessed=8 << 20, transcendentals=0),
        name="kept_half",
    )(turned, halo, wide)

    mine, low, high_lanes = pl.pallas_call(
        pair_kernel,
        out_shape=(
            shape((kept_rows, MINE), F32),
            shape((kept_rows, LOW), BF16),
            shape((kept_rows, HIGH), BF16),
        ),
        in_specs=[vmem] * 2,
        out_specs=(vmem,) * 3,
        compiler_params=params,
        name="pair_sum",
    )(keep, got)
    low = lax.ppermute(low, "sample", flipped(sample, 1))
    high_lanes = lax.ppermute(high_lanes, "sample", flipped(sample, sample // 2))
    own, *leaving = pl.pallas_call(
        cross_kernel,
        out_shape=(shape(part, F32),) + (shape(part, BF16),) * (depth - 1),
        in_specs=[vmem] * 3,
        out_specs=(vmem,) * depth,
        compiler_params=params,
        name="cross_sum",
    )(mine, low, high_lanes)
    came = [
        lax.ppermute(leaving[k - 1], "space", flipped(space, 2 * k))
        for k in reversed(range(1, depth))
    ]

    grad_in, done = pl.pallas_call(
        input_kernel,
        out_shape=(shape(x.shape, BF16), shape((8, 128), F32)),
        in_specs=[vmem] * 3,
        out_specs=(vmem, vmem),
        compiler_params=params,
        cost_estimate=pl.CostEstimate(flops=flops, bytes_accessed=8 << 20, transcendentals=0),
        name="input_grad",
    )(grad, below, band)

    total = pl.pallas_call(
        depth_kernel,
        out_shape=shape(part, BF16),
        in_specs=[vmem] * (depth + 1),
        out_specs=vmem,
        compiler_params=params,
        name="depth_sum",
    )(done, own, *came)
    others = [lax.ppermute(total, "sample", flipped(sample, j)) for j in range(1, sample)]
    kernel_grad = pl.pallas_call(
        functools.partial(sample_kernel, 1.0 / (samples * sample)),
        out_shape=shape((TAPS * 3, width, CIN), F32),
        in_specs=[vmem] * sample,
        out_specs=vmem,
        compiler_params=params,
        name="sample_sum",
    )(total, *others)
    kernel_grad = jnp.transpose(kernel_grad, (0, 2, 1)).reshape(3, 3, 3, CIN, width)
    return act.reshape(cotangent.shape), grad_in.reshape(slabs.shape), kernel_grad


def solution(mesh):
    placed = (P("sample", "space", None, None), P(), P("sample", "space", None, None))
    return jax.shard_map(
        per_device,
        mesh=mesh,
        in_specs=placed,
        out_specs=(
            P("sample", "space", None, None),
            P("sample", "space", None, None),
            P(None, None, None, None, "space"),
        ),
        check_vma=False,
    )
```

```python
import functools

import jax
import jax.numpy as jnp
from jax import lax
from jax.experimental import pallas as pl
from jax.experimental.pallas import tpu as pltpu
from jax.sharding import PartitionSpec as P

CIN = 96
COUT = 192
BLOCK = 384
SPAN = 512
TAPS = 9
LOW = 640
HIGH = 768
MINE = LOW + HIGH
F32 = jnp.float32
BF16 = jnp.bfloat16
VMEM_LIMIT = 12 * 1024 * 1024


def iota(shape, axis):
    return lax.broadcasted_iota(jnp.int32, shape, axis)


def row_split(planes):
    shape = (3 * planes * 16, planes * 32)
    row = iota(shape, 0)
    col = iota(shape, 1)
    j = row & 15
    plane = (row >> 4) & (planes - 1)
    b = jnp.where(row >= planes * 32, 2, jnp.where(row >= planes * 16, 1, 0))
    hit = (col == plane * 32 + 2 * j + b - 1) & ((j + b) > 0)
    return jnp.where(hit, 1.0, 0.0).astype(BF16)


def blank(rows, lanes):
    return jnp.zeros((rows, lanes), BF16)


def dot(lhs, rhs):
    return jnp.dot(lhs, rhs, preferred_element_type=F32)


def dot_nt(lhs, rhs):
    return lax.dot_general(lhs, rhs, (((1,), (1,)), ((), ())), preferred_element_type=F32)


def put(wide, per_out, cells, i, m, tap, piece):
    at = i * per_out + m * 16
    wide[at : at + 16, tap * SPAN + 128 : tap * SPAN + 512] = piece
    if m + 1 < cells:
        wide[at + 16 : at + 32, tap * SPAN : tap * SPAN + 128] = piece[:, 256:]
    if m == 0:
        wide[at : at + 16, tap * SPAN : tap * SPAN + 128] = jnp.zeros((16, 128), BF16)


def edge_kernel(width, x_hbm, edge_ref, split_ref, order_ref, sem):
    copy = pltpu.make_async_copy(x_hbm.at[x_hbm.shape[0] - 1], edge_ref, sem)
    copy.start()
    split_ref[...] = row_split(x_hbm.shape[0])
    at = lax.axis_index("space")
    core = at % 2
    chip = at // 2
    steps = lax.axis_size("space") // 2
    shape = order_ref.shape
    rows = shape[0] // 4
    high = rows // steps
    inner = iota(shape, 0)
    kept = inner >= 2 * rows
    inner = inner - jnp.where(kept, 2 * rows, 0)
    odd = inner >= rows
    inner = inner - jnp.where(odd, rows, 0)
    source = jnp.where(kept, core, 1 - core) * width + jnp.where(odd, COUT, 0)
    for k in range(steps):
        channel = inner - k * high
        inside = (channel >= 0) & (channel < width)
        source = source + jnp.where(inside, channel + (chip ^ k) * 2 * width, 0)
        if high != width:
            source = jnp.where((channel >= width) & (channel < high), -1, source)
    order_ref[...] = jnp.where(iota(shape, 1) == source, 1.0, 0.0).astype(BF16)
    copy.wait()


def by_parity(wide, even_band, odd_band, taps):
    sides = []
    for start, band in ((0, even_band), (SPAN - BLOCK, odd_band)):
        windows = [wide[:, tap * SPAN + start : tap * SPAN + start + BLOCK] for tap in range(taps)]
        sides.append(dot(jnp.concatenate(windows, axis=1), band[: taps * BLOCK]))
    return sides


def own_kernel(x_ref, split_ref, w_hbm, wide, even_band, odd_band, preact, w_ref, sem):
    planes = x_ref.shape[0]
    outs = planes // 2
    cells = x_ref.shape[2] // BLOCK
    per_out = cells * 16
    copy = pltpu.make_async_copy(w_hbm, w_ref, sem)
    copy.start()
    split = split_ref[...]
    wide[0:per_out, 0 : 3 * SPAN] = jnp.zeros((per_out, 3 * SPAN), BF16)
    x = x_ref[...].reshape(planes * 32, x_ref.shape[2])
    for m in range(cells):
        rows = dot(split, x[:, m * BLOCK : (m + 1) * BLOCK]).astype(BF16)
        for b in range(3):
            for p in range(planes):
                piece = rows[(b * planes + p) * 16 : (b * planes + p + 1) * 16]
                if p % 2 == 0:
                    put(wide, per_out, cells, p // 2, m, 3 + b, piece)
                else:
                    put(wide, per_out, cells, p // 2, m, 6 + b, piece)
                    if p // 2 + 1 < outs:
                        put(wide, per_out, cells, p // 2 + 1, m, b, piece)
    copy.wait()
    for tap in range(TAPS):
        at = tap * BLOCK
        even_band[at : at + 32] = blank(32, COUT)
        even_band[at + 32 : at + 320] = w_ref[tap]
        even_band[at + 320 : at + BLOCK] = blank(64, COUT)
        odd_band[at : at + 96] = blank(96, COUT)
        odd_band[at + 96 : at + BLOCK] = w_ref[tap]
    even, odd = by_parity(wide, even_band, odd_band, TAPS)
    preact[:, :COUT] = even
    preact[:, COUT:] = odd


def add_terms(turned, edge, wide, terms):
    rows = terms.shape[0]
    per_out = edge.shape[0]
    terms[...] = jnp.zeros_like(terms)
    lane = iota((rows, SPAN), 1)
    even_lanes = (lane >= 32) & (lane < 320)
    odd_lanes = lane >= 224
    for tap in range(TAPS):
        lanes = slice(tap * SPAN, (tap + 1) * SPAN)
        if tap < 3:
            cols = jnp.concatenate([edge[:, lanes], wide[per_out:, lanes]], axis=0)
        else:
            cols = wide[:, lanes]
        both = dot(turned, cols)
        base = tap * 288 // 128 * 128
        shift = tap * 288 - base
        even = jnp.where(even_lanes, both[:rows], 0.0)
        odd = jnp.where(odd_lanes, both[rows:], 0.0)
        even = pltpu.roll(even, (shift - 32) % SPAN, 1)
        odd = pltpu.roll(odd, (shift - 224) % SPAN, 1)
        terms[:, base : base + BLOCK] += (even + odd)[:, :BLOCK]


def halo_kernel(
    above_ref, order_ref, wide, even_band, odd_band, pre_ref, cot_ref,
    act_ref, gp_ref, first_ref, turned_ref, edge, send_ref, terms,
):
    outs = cot_ref.shape[0]
    cells = cot_ref.shape[2] // BLOCK
    per_out = cells * 16
    top = lax.axis_index("space") == 0
    split_one = row_split(1)
    for m in range(cells):
        lanes = slice(m * BLOCK, (m + 1) * BLOCK)
        plane = above_ref[:, lanes]
        plane = jnp.where(top, jnp.zeros_like(plane), plane)
        above = dot(split_one, plane).astype(BF16)
        for b in range(3):
            put(edge, per_out, cells, 0, m, b, above[b * 16 : b * 16 + 16])
    added = jnp.concatenate(by_parity(edge, even_band, odd_band, 3), axis=1)
    for i in range(outs):
        for m in range(cells):
            lanes = slice(m * BLOCK, (m + 1) * BLOCK)
            at = i * per_out + m * 16
            value = pre_ref[at : at + 16]
            if i == 0:
                value = value + added[at : at + 16]
            sig = jax.nn.sigmoid(value)
            act_ref[i, :, lanes] = (value * sig).astype(BF16)
            grad = cot_ref[i, :, lanes].astype(F32) * (sig * (1.0 + value * (1.0 - sig)))
            grad = grad.astype(BF16)
            gp_ref[at : at + 16] = grad
            if i == 0:
                first_ref[at : at + 16] = grad

    turned_ref[...] = dot_nt(order_ref[...], gp_ref[...]).astype(BF16)
    add_terms(turned_ref[: 2 * send_ref.shape[0]], edge, wide, terms)
    send_ref[...] = terms[...].astype(BF16)


def keep_kernel(turned_ref, edge, wide, keep_ref):
    add_terms(turned_ref[2 * keep_ref.shape[0] :], edge, wide, keep_ref)


def input_kernel(gp_ref, below_ref, w_ref, out_ref, done_ref, band):
    done_ref[...] = jnp.zeros_like(done_ref)
    for tap in range(TAPS):
        w = w_ref[tap]
        even = jnp.concatenate([blank(32, COUT), w, blank(192, COUT)], axis=0)
        odd = jnp.concatenate([blank(224, COUT), w], axis=0)
        band[tap * SPAN : (tap + 1) * SPAN] = jnp.concatenate([even, odd], axis=1)
    per_out = below_ref.shape[0]
    cells = per_out // 16
    here = gp_ref[...]
    following = below_ref[...]
    last = lax.axis_index("space") == lax.axis_size("space") - 1
    following = jnp.where(last, jnp.zeros_like(following), following)
    there = jnp.concatenate([here[per_out:], following], axis=0)
    count = gp_ref.shape[0]
    outs = count // per_out
    shape = (128, 128)
    row = iota(shape, 0)
    below = jnp.where((iota(shape, 1) == row + 1) & ((row & 15) != 15), 1.0, 0.0).astype(BF16)

    def lowered(block):
        return jnp.concatenate(
            [dot(below, block[at : at + 128]).astype(BF16) for at in range(0, count, 128)], axis=0
        )

    here_low = lowered(here)
    there_low = lowered(there)

    def term(grad, a, b):
        tap = a * 3 + b
        return dot_nt(grad, band[tap * SPAN : (tap + 1) * SPAN])

    groups = {
        (0, 0): term(here, 1, 1),
        (0, 1): term(here, 1, 2) + term(here_low, 1, 0),
        (1, 0): term(here, 2, 1) + term(there, 0, 1),
        (1, 1): term(here, 2, 2) + term(here_low, 2, 0) + term(there, 0, 2) + term(there_low, 0, 0),
    }
    shape = (32, 32)
    row = iota(shape, 0)
    weave = jnp.where(iota(shape, 1) == (row >> 1) + (row & 1) * 16, 1.0, 0.0).astype(BF16)
    for i in range(outs):
        for m in range(cells):
            at = i * per_out + m * 16
            for pd in range(2):
                parts = []
                for ph in range(2):
                    y = groups[pd, ph]
                    body = y[at : at + 16, 128:512]
                    if m + 1 < cells:
                        body = jnp.concatenate(
                            [body[:, :256], body[:, 256:] + y[at + 16 : at + 32, :128]], axis=1
                        )
                    parts.append(body.astype(BF16))
                mixed = dot(weave, jnp.concatenate(parts, axis=0)).astype(BF16)
                out_ref[2 * i + pd, :, m * BLOCK : (m + 1) * BLOCK] = mixed


def sample_bits():
    at = lax.axis_index("sample")
    return at % 2, at // (lax.axis_size("sample") // 2)


def pair_kernel(keep_ref, got_ref, mine_ref, low_ref, high_ref):
    def total(start, lanes):
        lanes = pl.ds(pl.multiple_of(start, 128), lanes)
        return keep_ref[:, lanes] + got_ref[:, lanes].astype(F32)

    low, high = sample_bits()
    low_ref[...] = total((1 - low) * LOW, LOW).astype(BF16)
    high_ref[...] = total(2 * LOW + (1 - high) * HIGH, HIGH).astype(BF16)
    mine_ref[:, :LOW] = total(low * LOW, LOW)
    mine_ref[:, LOW:] = total(2 * LOW + high * HIGH, HIGH)


def cross_kernel(mine_ref, low_ref, high_ref, *out_refs):
    for lanes, ref in ((slice(0, LOW), low_ref), (slice(LOW, MINE), high_ref)):
        total = mine_ref[:, lanes] + ref[...].astype(F32)
        high = out_refs[0].shape[0]
        for k, out_ref in enumerate(out_refs):
            out_ref[:, lanes] = total[k * high : (k + 1) * high].astype(out_ref.dtype)


def depth_kernel(done_ref, own_ref, *refs):
    del done_ref
    total = own_ref[...]
    for ref in refs[:-1]:
        total = total + ref[...].astype(F32)
    refs[-1][...] = total.astype(BF16)


def store_kernel(total_ref, *refs):
    del total_ref
    count = (len(refs) - 1) // 2
    sems = refs[-1]
    copies = [pltpu.make_async_copy(refs[n], refs[count + n], sems.at[n]) for n in range(count)]
    for copy in copies:
        copy.start()
    for copy in copies:
        copy.wait()


def tree(parts):
    while len(parts) > 1:
        parts = [parts[n] + parts[n + 1] for n in range(0, len(parts), 2)]
    return parts[0]


def sample_kernel(scale, *refs):
    out_ref = refs[-1]
    width = out_ref.shape[1]
    parts = [ref[...].astype(F32)[:width] * scale for ref in refs[:-1]]
    half = len(parts) // 2
    here = tree([part[:, :LOW] for part in parts[0::2]])
    there = tree([part[:, :LOW] for part in parts[1::2]])
    above = tree([part[:, LOW:] for part in parts[:half]])
    below = tree([part[:, LOW:] for part in parts[half:]])
    low, high = (bit == 0 for bit in sample_bits())
    total = jnp.concatenate(
        [
            jnp.where(low, here, there),
            jnp.where(low, there, here),
            jnp.where(high, above, below),
            jnp.where(high, below, above),
        ],
        axis=1,
    )
    for n in range(out_ref.shape[0]):
        out_ref[n] = total[:, n * CIN : (n + 1) * CIN]


def flipped(size, bits):
    return [(i, i ^ bits) for i in range(size)]


def per_device(slabs, weight, cotangent):
    samples, planes, rows, lanes = slabs.shape
    outs = planes // 2
    space = lax.axis_size("space")
    sample = lax.axis_size("sample")
    depth = space // 2
    width = COUT // space
    high = -(-width // 8) * 8
    kept_rows = depth * high
    terms = (kept_rows, 2 * MINE)
    part = (high, MINE)
    cells = lanes // BLOCK
    per_out = cells * 16
    count = outs * per_out

    in_chip = flipped(space, 1)
    onward = [(i, (i + 1) % space) for i in range(space)]
    back = [(b, a) for a, b in onward]

    x = slabs.reshape(planes, rows, lanes)
    cot = cotangent.reshape(outs, rows // 2, lanes)
    w = weight.reshape(TAPS, 3 * CIN, COUT)
    vmem = pl.BlockSpec(memory_space=pltpu.VMEM)
    hbm = pl.BlockSpec(memory_space=pltpu.HBM)
    params = pltpu.CompilerParams(vmem_limit_bytes=VMEM_LIMIT)
    shape = jax.ShapeDtypeStruct
    flops = 2 * count * TAPS * SPAN * BLOCK

    edge, split, order = pl.pallas_call(
        functools.partial(edge_kernel, width),
        out_shape=(
            shape((rows, lanes), BF16),
            shape((3 * planes * 16, planes * 32), BF16),
            shape((4 * kept_rows, 2 * COUT), BF16),
        ),
        in_specs=[hbm],
        out_specs=(vmem,) * 3,
        scratch_shapes=[pltpu.SemaphoreType.DMA(())],
        compiler_params=params,
        cost_estimate=pl.CostEstimate(flops=0, bytes_accessed=10 << 20, transcendentals=0),
        name="edge_plane",
    )(pltpu.with_memory_space_constraint(x, pltpu.HBM))
    above = lax.ppermute(edge, "space", onward)
    wide, even_band, odd_band, preact, w_in = pl.pallas_call(
        own_kernel,
        out_shape=(
            shape((count, TAPS * SPAN), BF16),
            shape((TAPS * BLOCK, COUT), BF16),
            shape((TAPS * BLOCK, COUT), BF16),
            shape((count, BLOCK), F32),
            shape(w.shape, BF16),
        ),
        in_specs=[vmem, vmem, hbm],
        out_specs=(vmem,) * 5,
        scratch_shapes=[pltpu.SemaphoreType.DMA(())],
        compiler_params=params,
        cost_estimate=pl.CostEstimate(flops=flops, bytes_accessed=12 << 20, transcendentals=0),
        name="own_planes",
    )(x, split, pltpu.with_memory_space_constraint(w, pltpu.HBM))

    act, grad, first, turned, halo, send = pl.pallas_call(
        halo_kernel,
        out_shape=(
            shape(cot.shape, BF16),
            shape((count, BLOCK), BF16),
            shape((per_out, BLOCK), BF16),
            shape((4 * kept_rows, count), BF16),
            shape((per_out, 3 * SPAN), BF16),
            shape(terms, BF16),
        ),
        in_specs=[vmem] * 7,
        out_specs=(vmem,) * 6,
        scratch_shapes=[pltpu.VMEM(terms, F32)],
        compiler_params=params,
        cost_estimate=pl.CostEstimate(
            flops=flops // 2, bytes_accessed=8 << 20, transcendentals=count * BLOCK
        ),
        name="halo_and_sent_half",
    )(above, order, wide, even_band, odd_band, preact, cot)
    got = lax.ppermute(send, "space", in_chip)
    below = lax.ppermute(first, "space", back)
    keep = pl.pallas_call(
        keep_kernel,
        out_shape=shape(terms, F32),
        in_specs=[vmem] * 3,
        out_specs=vmem,
        compiler_params=params,
        cost_estimate=pl.CostEstimate(flops=flops // 2, bytes_accessed=8 << 20, transcendentals=0),
        name="kept_half",
    )(turned, halo, wide)

    mine, low, high_lanes = pl.pallas_call(
        pair_kernel,
        out_shape=(
            shape((kept_rows, MINE), F32),
            shape((kept_rows, LOW), BF16),
            shape((kept_rows, HIGH), BF16),
        ),
        in_specs=[vmem] * 2,
        out_specs=(vmem,) * 3,
        compiler_params=params,
        name="pair_sum",
    )(keep, got)
    low = lax.ppermute(low, "sample", flipped(sample, 1))
    high_lanes = lax.ppermute(high_lanes, "sample", flipped(sample, sample // 2))
    own, *leaving = pl.pallas_call(
        cross_kernel,
        out_shape=(shape(part, F32),) + (shape(part, BF16),) * (depth - 1),
        in_specs=[vmem] * 3,
        out_specs=(vmem,) * depth,
        compiler_params=params,
        name="cross_sum",
    )(mine, low, high_lanes)
    came = [
        lax.ppermute(leaving[k - 1], "space", flipped(space, 2 * k))
        for k in reversed(range(1, depth))
    ]

    grad_in, done = pl.pallas_call(
        input_kernel,
        out_shape=(shape(x.shape, BF16), shape((8, 128), F32)),
        in_specs=[vmem] * 3,
        out_specs=(vmem, vmem),
        scratch_shapes=[pltpu.VMEM((TAPS * SPAN, BLOCK), BF16)],
        compiler_params=params,
        cost_estimate=pl.CostEstimate(flops=flops, bytes_accessed=8 << 20, transcendentals=0),
        name="input_grad",
    )(grad, below, w_in)

    total = pl.pallas_call(
        depth_kernel,
        out_shape=shape(part, BF16),
        in_specs=[vmem] * (depth + 1),
        out_specs=vmem,
        compiler_params=params,
        name="depth_sum",
    )(done, own, *came)
    act, grad_in = pl.pallas_call(
        store_kernel,
        out_shape=(shape(cot.shape, BF16), shape(x.shape, BF16)),
        in_specs=[vmem] * 3,
        out_specs=(hbm, hbm),
        scratch_shapes=[pltpu.SemaphoreType.DMA((2,))],
        compiler_params=params,
        name="store",
    )(total, act, grad_in)
    others = [lax.ppermute(total, "sample", flipped(sample, j)) for j in range(1, sample)]
    kernel_grad = pl.pallas_call(
        functools.partial(sample_kernel, 1.0 / (samples * sample)),
        out_shape=shape((TAPS * 3, width, CIN), F32),
        in_specs=[vmem] * sample,
        out_specs=vmem,
        compiler_params=params,
        name="sample_sum",
    )(total, *others)
    kernel_grad = jnp.transpose(kernel_grad, (0, 2, 1)).reshape(3, 3, 3, CIN, width)
    return act.reshape(cotangent.shape), grad_in.reshape(slabs.shape), kernel_grad


def solution(mesh):
    placed = (P("sample", "space", None, None), P(), P("sample", "space", None, None))
    return jax.shard_map(
        per_device,
        mesh=mesh,
        in_specs=placed,
        out_specs=(
            P("sample", "space", None, None),
            P("sample", "space", None, None),
            P(None, None, None, None, "space"),
        ),
        check_vma=False,
    )
```

```python
import functools

import jax
import jax.numpy as jnp
from jax import lax
from jax.experimental import pallas as pl
from jax.experimental.pallas import tpu as pltpu
from jax.sharding import PartitionSpec as P

CIN = 96
COUT = 192
BLOCK = 384
SPAN = 512
TAPS = 9
LOW = 640
HIGH = 768
MINE = LOW + HIGH
F32 = jnp.float32
BF16 = jnp.bfloat16
VMEM_LIMIT = 12 * 1024 * 1024


def iota(shape, axis):
    return lax.broadcasted_iota(jnp.int32, shape, axis)


def row_split(planes):
    shape = (3 * planes * 16, planes * 32)
    row = iota(shape, 0)
    col = iota(shape, 1)
    j = row & 15
    plane = (row >> 4) & (planes - 1)
    b = jnp.where(row >= planes * 32, 2, jnp.where(row >= planes * 16, 1, 0))
    hit = (col == plane * 32 + 2 * j + b - 1) & ((j + b) > 0)
    return jnp.where(hit, 1.0, 0.0).astype(BF16)


def blank(rows, lanes):
    return jnp.zeros((rows, lanes), BF16)


def dot(lhs, rhs):
    return jnp.dot(lhs, rhs, preferred_element_type=F32)


def dot_nt(lhs, rhs):
    return lax.dot_general(lhs, rhs, (((1,), (1,)), ((), ())), preferred_element_type=F32)


def put(wide, per_out, cells, i, m, tap, piece):
    at = i * per_out + m * 16
    wide[at : at + 16, tap * SPAN + 128 : tap * SPAN + 512] = piece
    if m + 1 < cells:
        wide[at + 16 : at + 32, tap * SPAN : tap * SPAN + 128] = piece[:, 256:]
    if m == 0:
        wide[at : at + 16, tap * SPAN : tap * SPAN + 128] = jnp.zeros((16, 128), BF16)


def edge_kernel(width, x_hbm, edge_ref, split_ref, order_ref, sem):
    copy = pltpu.make_async_copy(x_hbm.at[x_hbm.shape[0] - 1], edge_ref, sem)
    copy.start()
    split_ref[...] = row_split(x_hbm.shape[0])
    at = lax.axis_index("space")
    core = at % 2
    chip = at // 2
    steps = lax.axis_size("space") // 2
    shape = order_ref.shape
    rows = shape[0] // 4
    high = rows // steps
    inner = iota(shape, 0)
    kept = inner >= 2 * rows
    inner = inner - jnp.where(kept, 2 * rows, 0)
    odd = inner >= rows
    inner = inner - jnp.where(odd, rows, 0)
    source = jnp.where(kept, core, 1 - core) * width + jnp.where(odd, COUT, 0)
    for k in range(steps):
        channel = inner - k * high
        inside = (channel >= 0) & (channel < width)
        source = source + jnp.where(inside, channel + (chip ^ k) * 2 * width, 0)
        if high != width:
            source = jnp.where((channel >= width) & (channel < high), -1, source)
    order_ref[...] = jnp.where(iota(shape, 1) == source, 1.0, 0.0).astype(BF16)
    copy.wait()


def by_parity(wide, even_band, odd_band, taps):
    sides = []
    for start, band in ((0, even_band), (SPAN - BLOCK, odd_band)):
        windows = [wide[:, tap * SPAN + start : tap * SPAN + start + BLOCK] for tap in range(taps)]
        sides.append(dot(jnp.concatenate(windows, axis=1), band[: taps * BLOCK]))
    return sides


def activate(value, cot):
    sig = jax.nn.sigmoid(value)
    grad = cot.astype(F32) * (sig * (1.0 + value * (1.0 - sig)))
    return (value * sig).astype(BF16), grad.astype(BF16)


def own_kernel(
    x_ref, split_ref, order_ref, w_hbm, cot_hbm,
    wide, even_band, odd_band, pre_ref, act_ref, gp_ref, turned_ref, cot_ref, w_ref,
    preact, sems,
):
    planes = x_ref.shape[0]
    outs = planes // 2
    cells = x_ref.shape[2] // BLOCK
    per_out = cells * 16
    w_copy = pltpu.make_async_copy(w_hbm, w_ref, sems.at[0])
    cot_copy = pltpu.make_async_copy(cot_hbm, cot_ref, sems.at[1])
    w_copy.start()
    cot_copy.start()
    split = split_ref[...]
    wide[0:per_out, 0 : 3 * SPAN] = jnp.zeros((per_out, 3 * SPAN), BF16)
    x = x_ref[...].reshape(planes * 32, x_ref.shape[2])
    for m in range(cells):
        rows = dot(split, x[:, m * BLOCK : (m + 1) * BLOCK]).astype(BF16)
        for b in range(3):
            for p in range(planes):
                piece = rows[(b * planes + p) * 16 : (b * planes + p + 1) * 16]
                if p % 2 == 0:
                    put(wide, per_out, cells, p // 2, m, 3 + b, piece)
                else:
                    put(wide, per_out, cells, p // 2, m, 6 + b, piece)
                    if p // 2 + 1 < outs:
                        put(wide, per_out, cells, p // 2 + 1, m, b, piece)
    w_copy.wait()
    for tap in range(TAPS):
        at = tap * BLOCK
        even_band[at : at + 32] = blank(32, COUT)
        even_band[at + 32 : at + 320] = w_ref[tap]
        even_band[at + 320 : at + BLOCK] = blank(64, COUT)
        odd_band[at : at + 96] = blank(96, COUT)
        odd_band[at + 96 : at + BLOCK] = w_ref[tap]
    even, odd = by_parity(wide, even_band, odd_band, TAPS)
    preact[:, :COUT] = even
    preact[:, COUT:] = odd
    pre_ref[...] = preact[:per_out]
    cot_copy.wait()
    for i in range(1, outs):
        for m in range(cells):
            lanes = slice(m * BLOCK, (m + 1) * BLOCK)
            at = i * per_out + m * 16
            act, grad = activate(preact[at : at + 16], cot_ref[i, :, lanes])
            act_ref[i - 1, :, lanes] = act
            gp_ref[at - per_out : at - per_out + 16] = grad
    turned_ref[...] = dot_nt(order_ref[...], gp_ref[...]).astype(BF16)


def add_terms(turned, edge, wide, terms):
    rows = terms.shape[0]
    per_out = edge.shape[0]
    terms[...] = jnp.zeros_like(terms)
    lane = iota((rows, SPAN), 1)
    even_lanes = (lane >= 32) & (lane < 320)
    odd_lanes = lane >= 224
    for tap in range(TAPS):
        lanes = slice(tap * SPAN, (tap + 1) * SPAN)
        if tap < 3:
            cols = jnp.concatenate([edge[:, lanes], wide[per_out:, lanes]], axis=0)
        else:
            cols = wide[:, lanes]
        both = dot(turned, cols)
        base = tap * 288 // 128 * 128
        shift = tap * 288 - base
        even = jnp.where(even_lanes, both[:rows], 0.0)
        odd = jnp.where(odd_lanes, both[rows:], 0.0)
        even = pltpu.roll(even, (shift - 32) % SPAN, 1)
        odd = pltpu.roll(odd, (shift - 224) % SPAN, 1)
        terms[:, base : base + BLOCK] += (even + odd)[:, :BLOCK]


def halo_kernel(
    above_ref, order_ref, wide, even_band, odd_band, pre_ref, cot_ref, rest_ref,
    act_ref, gp_ref, turned_ref, edge, send_ref, terms,
):
    cells = cot_ref.shape[2] // BLOCK
    per_out = cells * 16
    top = lax.axis_index("space") == 0
    split_one = row_split(1)
    for m in range(cells):
        lanes = slice(m * BLOCK, (m + 1) * BLOCK)
        plane = above_ref[:, lanes]
        plane = jnp.where(top, jnp.zeros_like(plane), plane)
        above = dot(split_one, plane).astype(BF16)
        for b in range(3):
            put(edge, per_out, cells, 0, m, b, above[b * 16 : b * 16 + 16])
    value = pre_ref[...] + jnp.concatenate(by_parity(edge, even_band, odd_band, 3), axis=1)
    for m in range(cells):
        lanes = slice(m * BLOCK, (m + 1) * BLOCK)
        rows = slice(m * 16, m * 16 + 16)
        act_ref[:, lanes], gp_ref[rows] = activate(value[rows], cot_ref[0, :, lanes])
    turned_ref[:, :per_out] = dot_nt(order_ref[...], gp_ref[...]).astype(BF16)
    turned_ref[:, per_out:] = rest_ref[...]
    add_terms(turned_ref[: 2 * send_ref.shape[0]], edge, wide, terms)
    send_ref[...] = terms[...].astype(BF16)


def keep_kernel(turned_ref, edge, wide, keep_ref):
    add_terms(turned_ref[2 * keep_ref.shape[0] :], edge, wide, keep_ref)


def input_kernel(gp_ref, rest_ref, below_ref, w_ref, out_ref, done_ref, band):
    done_ref[...] = jnp.zeros_like(done_ref)
    for tap in range(TAPS):
        w = w_ref[tap]
        even = jnp.concatenate([blank(32, COUT), w, blank(192, COUT)], axis=0)
        odd = jnp.concatenate([blank(224, COUT), w], axis=0)
        band[tap * SPAN : (tap + 1) * SPAN] = jnp.concatenate([even, odd], axis=1)
    per_out = below_ref.shape[0]
    cells = per_out // 16
    here = jnp.concatenate([gp_ref[...], rest_ref[...]], axis=0)
    following = below_ref[...]
    last = lax.axis_index("space") == lax.axis_size("space") - 1
    following = jnp.where(last, jnp.zeros_like(following), following)
    there = jnp.concatenate([here[per_out:], following], axis=0)
    count = here.shape[0]
    outs = count // per_out
    shape = (128, 128)
    row = iota(shape, 0)
    below = jnp.where((iota(shape, 1) == row + 1) & ((row & 15) != 15), 1.0, 0.0).astype(BF16)

    def lowered(block):
        return jnp.concatenate(
            [dot(below, block[at : at + 128]).astype(BF16) for at in range(0, count, 128)], axis=0
        )

    here_low = lowered(here)
    there_low = lowered(there)

    def term(grad, a, b):
        tap = a * 3 + b
        return dot_nt(grad, band[tap * SPAN : (tap + 1) * SPAN])

    groups = {
        (0, 0): term(here, 1, 1),
        (0, 1): term(here, 1, 2) + term(here_low, 1, 0),
        (1, 0): term(here, 2, 1) + term(there, 0, 1),
        (1, 1): term(here, 2, 2) + term(here_low, 2, 0) + term(there, 0, 2) + term(there_low, 0, 0),
    }
    shape = (32, 32)
    row = iota(shape, 0)
    weave = jnp.where(iota(shape, 1) == (row >> 1) + (row & 1) * 16, 1.0, 0.0).astype(BF16)
    for i in range(outs):
        for m in range(cells):
            at = i * per_out + m * 16
            for pd in range(2):
                parts = []
                for ph in range(2):
                    y = groups[pd, ph]
                    body = y[at : at + 16, 128:512]
                    if m + 1 < cells:
                        body = jnp.concatenate(
                            [body[:, :256], body[:, 256:] + y[at + 16 : at + 32, :128]], axis=1
                        )
                    parts.append(body.astype(BF16))
                mixed = dot(weave, jnp.concatenate(parts, axis=0)).astype(BF16)
                out_ref[2 * i + pd, :, m * BLOCK : (m + 1) * BLOCK] = mixed


def sample_bits():
    at = lax.axis_index("sample")
    return at % 2, at // (lax.axis_size("sample") // 2)


def pair_kernel(keep_ref, got_ref, mine_ref, low_ref, high_ref):
    def total(start, lanes):
        lanes = pl.ds(pl.multiple_of(start, 128), lanes)
        return keep_ref[:, lanes] + got_ref[:, lanes].astype(F32)

    low, high = sample_bits()
    low_ref[...] = total((1 - low) * LOW, LOW).astype(BF16)
    high_ref[...] = total(2 * LOW + (1 - high) * HIGH, HIGH).astype(BF16)
    mine_ref[:, :LOW] = total(low * LOW, LOW)
    mine_ref[:, LOW:] = total(2 * LOW + high * HIGH, HIGH)


def cross_kernel(mine_ref, low_ref, high_ref, *out_refs):
    for lanes, ref in ((slice(0, LOW), low_ref), (slice(LOW, MINE), high_ref)):
        total = mine_ref[:, lanes] + ref[...].astype(F32)
        high = out_refs[0].shape[0]
        for k, out_ref in enumerate(out_refs):
            out_ref[:, lanes] = total[k * high : (k + 1) * high].astype(out_ref.dtype)


def depth_kernel(done_ref, own_ref, *refs):
    del done_ref
    total = own_ref[...]
    for ref in refs[:-1]:
        total = total + ref[...].astype(F32)
    refs[-1][...] = total.astype(BF16)


def store_kernel(total_ref, first_ref, rest_ref, grad_ref, act_hbm, grad_hbm, sems):
    del total_ref
    copies = [
        pltpu.make_async_copy(source, target, sems.at[n])
        for n, (source, target) in enumerate(
            (
                (grad_ref, grad_hbm),
                (rest_ref, act_hbm.at[pl.ds(1, rest_ref.shape[0])]),
                (first_ref, act_hbm.at[0]),
            )
        )
    ]
    for copy in copies:
        copy.start()
    for copy in copies:
        copy.wait()


def tree(parts):
    while len(parts) > 1:
        parts = [parts[n] + parts[n + 1] for n in range(0, len(parts), 2)]
    return parts[0]


def sample_kernel(scale, *refs):
    out_ref = refs[-1]
    width = out_ref.shape[1]
    parts = [ref[...].astype(F32)[:width] * scale for ref in refs[:-1]]
    half = len(parts) // 2
    here = tree([part[:, :LOW] for part in parts[0::2]])
    there = tree([part[:, :LOW] for part in parts[1::2]])
    above = tree([part[:, LOW:] for part in parts[:half]])
    below = tree([part[:, LOW:] for part in parts[half:]])
    low, high = (bit == 0 for bit in sample_bits())
    total = jnp.concatenate(
        [
            jnp.where(low, here, there),
            jnp.where(low, there, here),
            jnp.where(high, above, below),
            jnp.where(high, below, above),
        ],
        axis=1,
    )
    for n in range(out_ref.shape[0]):
        out_ref[n] = total[:, n * CIN : (n + 1) * CIN]


def flipped(size, bits):
    return [(i, i ^ bits) for i in range(size)]


def per_device(slabs, weight, cotangent):
    samples, planes, rows, lanes = slabs.shape
    outs = planes // 2
    space = lax.axis_size("space")
    sample = lax.axis_size("sample")
    depth = space // 2
    width = COUT // space
    high = -(-width // 8) * 8
    kept_rows = depth * high
    terms = (kept_rows, 2 * MINE)
    part = (high, MINE)
    cells = lanes // BLOCK
    per_out = cells * 16
    count = outs * per_out

    in_chip = flipped(space, 1)
    onward = [(i, (i + 1) % space) for i in range(space)]
    back = [(b, a) for a, b in onward]

    x = slabs.reshape(planes, rows, lanes)
    cot = cotangent.reshape(outs, rows // 2, lanes)
    w = weight.reshape(TAPS, 3 * CIN, COUT)
    vmem = pl.BlockSpec(memory_space=pltpu.VMEM)
    hbm = pl.BlockSpec(memory_space=pltpu.HBM)
    params = pltpu.CompilerParams(vmem_limit_bytes=VMEM_LIMIT)
    shape = jax.ShapeDtypeStruct
    flops = 2 * count * TAPS * SPAN * BLOCK

    edge, split, order = pl.pallas_call(
        functools.partial(edge_kernel, width),
        out_shape=(
            shape((rows, lanes), BF16),
            shape((3 * planes * 16, planes * 32), BF16),
            shape((4 * kept_rows, 2 * COUT), BF16),
        ),
        in_specs=[hbm],
        out_specs=(vmem,) * 3,
        scratch_shapes=[pltpu.SemaphoreType.DMA(())],
        compiler_params=params,
        cost_estimate=pl.CostEstimate(flops=0, bytes_accessed=10 << 20, transcendentals=0),
        name="edge_plane",
    )(pltpu.with_memory_space_constraint(x, pltpu.HBM))
    above = lax.ppermute(edge, "space", onward)
    wide, even_band, odd_band, preact, act, grad, rest, cot_in, w_in = pl.pallas_call(
        own_kernel,
        out_shape=(
            shape((count, TAPS * SPAN), BF16),
            shape((TAPS * BLOCK, COUT), BF16),
            shape((TAPS * BLOCK, COUT), BF16),
            shape((per_out, BLOCK), F32),
            shape((outs - 1,) + cot.shape[1:], BF16),
            shape((count - per_out, BLOCK), BF16),
            shape((4 * kept_rows, count - per_out), BF16),
            shape(cot.shape, BF16),
            shape(w.shape, BF16),
        ),
        in_specs=[vmem] * 3 + [hbm] * 2,
        out_specs=(vmem,) * 9,
        scratch_shapes=[pltpu.VMEM((count, BLOCK), F32), pltpu.SemaphoreType.DMA((2,))],
        compiler_params=params,
        cost_estimate=pl.CostEstimate(
            flops=flops, bytes_accessed=12 << 20, transcendentals=count * BLOCK
        ),
        name="own_planes",
    )(
        x,
        split,
        order,
        pltpu.with_memory_space_constraint(w, pltpu.HBM),
        pltpu.with_memory_space_constraint(cot, pltpu.HBM),
    )

    act_first, first, turned, halo, send = pl.pallas_call(
        halo_kernel,
        out_shape=(
            shape(cot.shape[1:], BF16),
            shape((per_out, BLOCK), BF16),
            shape((4 * kept_rows, count), BF16),
            shape((per_out, 3 * SPAN), BF16),
            shape(terms, BF16),
        ),
        in_specs=[vmem] * 8,
        out_specs=(vmem,) * 5,
        scratch_shapes=[pltpu.VMEM(terms, F32)],
        compiler_params=params,
        cost_estimate=pl.CostEstimate(
            flops=flops // 2, bytes_accessed=8 << 20, transcendentals=per_out * BLOCK
        ),
        name="halo_and_sent_half",
    )(above, order, wide, even_band, odd_band, preact, cot_in, rest)
    got = lax.ppermute(send, "space", in_chip)
    below = lax.ppermute(first, "space", back)
    keep = pl.pallas_call(
        keep_kernel,
        out_shape=shape(terms, F32),
        in_specs=[vmem] * 3,
        out_specs=vmem,
        compiler_params=params,
        cost_estimate=pl.CostEstimate(flops=flops // 2, bytes_accessed=8 << 20, transcendentals=0),
        name="kept_half",
    )(turned, halo, wide)

    mine, low, high_lanes = pl.pallas_call(
        pair_kernel,
        out_shape=(
            shape((kept_rows, MINE), F32),
            shape((kept_rows, LOW), BF16),
            shape((kept_rows, HIGH), BF16),
        ),
        in_specs=[vmem] * 2,
        out_specs=(vmem,) * 3,
        compiler_params=params,
        name="pair_sum",
    )(keep, got)
    low = lax.ppermute(low, "sample", flipped(sample, 1))
    high_lanes = lax.ppermute(high_lanes, "sample", flipped(sample, sample // 2))
    own, *leaving = pl.pallas_call(
        cross_kernel,
        out_shape=(shape(part, F32),) + (shape(part, BF16),) * (depth - 1),
        in_specs=[vmem] * 3,
        out_specs=(vmem,) * depth,
        compiler_params=params,
        name="cross_sum",
    )(mine, low, high_lanes)
    came = [
        lax.ppermute(leaving[k - 1], "space", flipped(space, 2 * k))
        for k in [*range(depth // 2, depth), *range(1, depth // 2)]
    ]

    grad_in, done = pl.pallas_call(
        input_kernel,
        out_shape=(shape(x.shape, BF16), shape((8, 128), F32)),
        in_specs=[vmem] * 4,
        out_specs=(vmem, vmem),
        scratch_shapes=[pltpu.VMEM((TAPS * SPAN, BLOCK), BF16)],
        compiler_params=params,
        cost_estimate=pl.CostEstimate(flops=flops, bytes_accessed=8 << 20, transcendentals=0),
        name="input_grad",
    )(first, grad, below, w_in)

    total = pl.pallas_call(
        depth_kernel,
        out_shape=shape(part, BF16),
        in_specs=[vmem] * (depth + 1),
        out_specs=vmem,
        compiler_params=params,
        name="depth_sum",
    )(done, own, *came)
    act, grad_in = pl.pallas_call(
        store_kernel,
        out_shape=(shape(cot.shape, BF16), shape(x.shape, BF16)),
        in_specs=[vmem] * 4,
        out_specs=(hbm, hbm),
        scratch_shapes=[pltpu.SemaphoreType.DMA((3,))],
        compiler_params=params,
        name="store",
    )(total, act_first, act, grad_in)
    others = [lax.ppermute(total, "sample", flipped(sample, j)) for j in range(1, sample)]
    kernel_grad = pl.pallas_call(
        functools.partial(sample_kernel, 1.0 / (samples * sample)),
        out_shape=shape((TAPS * 3, width, CIN), F32),
        in_specs=[vmem] * sample,
        out_specs=vmem,
        compiler_params=params,
        name="sample_sum",
    )(total, *others)
    kernel_grad = jnp.transpose(kernel_grad, (0, 2, 1)).reshape(3, 3, 3, CIN, width)
    return act.reshape(cotangent.shape), grad_in.reshape(slabs.shape), kernel_grad


def solution(mesh):
    placed = (P("sample", "space", None, None), P(), P("sample", "space", None, None))
    return jax.shard_map(
        per_device,
        mesh=mesh,
        in_specs=placed,
        out_specs=(
            P("sample", "space", None, None),
            P("sample", "space", None, None),
            P(None, None, None, None, "space"),
        ),
        check_vma=False,
    )
```

```python
import functools

import jax
import jax.numpy as jnp
from jax import lax
from jax.experimental import pallas as pl
from jax.experimental.pallas import tpu as pltpu
from jax.sharding import PartitionSpec as P

CIN = 96
COUT = 192
BLOCK = 384
SPAN = 512
TAPS = 9
SIDE = 640
REST = 4 * SIDE
TERMS = REST + 128
LEFT = TAPS * 3 * CIN - REST
F32 = jnp.float32
BF16 = jnp.bfloat16
VMEM_LIMIT = 12 * 1024 * 1024


def iota(shape, axis):
    return lax.broadcasted_iota(jnp.int32, shape, axis)


def row_split(planes):
    shape = (3 * planes * 16, planes * 32)
    row = iota(shape, 0)
    col = iota(shape, 1)
    j = row & 15
    plane = (row >> 4) & (planes - 1)
    b = jnp.where(row >= planes * 32, 2, jnp.where(row >= planes * 16, 1, 0))
    hit = (col == plane * 32 + 2 * j + b - 1) & ((j + b) > 0)
    return jnp.where(hit, 1.0, 0.0).astype(BF16)


def blank(rows, lanes):
    return jnp.zeros((rows, lanes), BF16)


def dot(lhs, rhs):
    return jnp.dot(lhs, rhs, preferred_element_type=F32)


def dot_nt(lhs, rhs):
    return lax.dot_general(lhs, rhs, (((1,), (1,)), ((), ())), preferred_element_type=F32)


def put(wide, per_out, cells, i, m, tap, piece):
    at = i * per_out + m * 16
    wide[at : at + 16, tap * SPAN + 128 : tap * SPAN + 512] = piece
    if m + 1 < cells:
        wide[at + 16 : at + 32, tap * SPAN : tap * SPAN + 128] = piece[:, 256:]
    if m == 0:
        wide[at : at + 16, tap * SPAN : tap * SPAN + 128] = jnp.zeros((16, 128), BF16)


def edge_kernel(width, x_hbm, edge_ref, split_ref, order_ref, sem):
    copy = pltpu.make_async_copy(x_hbm.at[x_hbm.shape[0] - 1], edge_ref, sem)
    copy.start()
    split_ref[...] = row_split(x_hbm.shape[0])
    at = lax.axis_index("space")
    core = at % 2
    chip = at // 2
    steps = lax.axis_size("space") // 2
    shape = order_ref.shape
    rows = shape[0] // 4
    high = rows // steps
    inner = iota(shape, 0)
    kept = inner >= 2 * rows
    inner = inner - jnp.where(kept, 2 * rows, 0)
    odd = inner >= rows
    inner = inner - jnp.where(odd, rows, 0)
    source = jnp.where(kept, core, 1 - core) * width + jnp.where(odd, COUT, 0)
    for k in range(steps):
        channel = inner - k * high
        inside = (channel >= 0) & (channel < width)
        source = source + jnp.where(inside, channel + (chip ^ k) * 2 * width, 0)
        if high != width:
            source = jnp.where((channel >= width) & (channel < high), -1, source)
    order_ref[...] = jnp.where(iota(shape, 1) == source, 1.0, 0.0).astype(BF16)
    copy.wait()


def by_parity(wide, even_band, odd_band, taps):
    sides = []
    for start, band in ((0, even_band), (SPAN - BLOCK, odd_band)):
        windows = [wide[:, tap * SPAN + start : tap * SPAN + start + BLOCK] for tap in range(taps)]
        sides.append(dot(jnp.concatenate(windows, axis=1), band[: taps * BLOCK]))
    return sides


def own_kernel(x_ref, split_ref, w_hbm, wide, even_band, odd_band, preact, w_ref, sem):
    planes = x_ref.shape[0]
    outs = planes // 2
    cells = x_ref.shape[2] // BLOCK
    per_out = cells * 16
    copy = pltpu.make_async_copy(w_hbm, w_ref, sem)
    copy.start()
    split = split_ref[...]
    wide[0:per_out, 0 : 3 * SPAN] = jnp.zeros((per_out, 3 * SPAN), BF16)
    x = x_ref[...].reshape(planes * 32, x_ref.shape[2])
    for m in range(cells):
        rows = dot(split, x[:, m * BLOCK : (m + 1) * BLOCK]).astype(BF16)
        for b in range(3):
            for p in range(planes):
                piece = rows[(b * planes + p) * 16 : (b * planes + p + 1) * 16]
                if p % 2 == 0:
                    put(wide, per_out, cells, p // 2, m, 3 + b, piece)
                else:
                    put(wide, per_out, cells, p // 2, m, 6 + b, piece)
                    if p // 2 + 1 < outs:
                        put(wide, per_out, cells, p // 2 + 1, m, b, piece)
    copy.wait()
    for tap in range(TAPS):
        at = tap * BLOCK
        even_band[at : at + 32] = blank(32, COUT)
        even_band[at + 32 : at + 320] = w_ref[tap]
        even_band[at + 320 : at + BLOCK] = blank(64, COUT)
        odd_band[at : at + 96] = blank(96, COUT)
        odd_band[at + 96 : at + BLOCK] = w_ref[tap]
    even, odd = by_parity(wide, even_band, odd_band, TAPS)
    preact[:, :COUT] = even
    preact[:, COUT:] = odd


def add_terms(turned, edge, wide, terms):
    rows = terms.shape[0]
    per_out = edge.shape[0]
    terms[...] = jnp.zeros_like(terms)
    lane = iota((rows, SPAN), 1)
    even_lanes = (lane >= 32) & (lane < 320)
    odd_lanes = lane >= 224
    for tap in range(TAPS):
        lanes = slice(tap * SPAN, (tap + 1) * SPAN)
        if tap < 3:
            cols = jnp.concatenate([edge[:, lanes], wide[per_out:, lanes]], axis=0)
        else:
            cols = wide[:, lanes]
        both = dot(turned, cols)
        base = tap * 288 // 128 * 128
        shift = tap * 288 - base
        even = jnp.where(even_lanes, both[:rows], 0.0)
        odd = jnp.where(odd_lanes, both[rows:], 0.0)
        even = pltpu.roll(even, (shift - 32) % SPAN, 1)
        odd = pltpu.roll(odd, (shift - 224) % SPAN, 1)
        terms[:, base : base + BLOCK] += (even + odd)[:, :BLOCK]


def halo_kernel(
    above_ref, order_ref, wide, even_band, odd_band, pre_ref, cot_ref,
    act_ref, gp_ref, first_ref, turned_ref, edge, send_ref, terms,
):
    outs = cot_ref.shape[0]
    cells = cot_ref.shape[2] // BLOCK
    per_out = cells * 16
    top = lax.axis_index("space") == 0
    split_one = row_split(1)
    for m in range(cells):
        lanes = slice(m * BLOCK, (m + 1) * BLOCK)
        plane = above_ref[:, lanes]
        plane = jnp.where(top, jnp.zeros_like(plane), plane)
        above = dot(split_one, plane).astype(BF16)
        for b in range(3):
            put(edge, per_out, cells, 0, m, b, above[b * 16 : b * 16 + 16])
    added = jnp.concatenate(by_parity(edge, even_band, odd_band, 3), axis=1)
    for i in range(outs):
        for m in range(cells):
            lanes = slice(m * BLOCK, (m + 1) * BLOCK)
            at = i * per_out + m * 16
            value = pre_ref[at : at + 16]
            if i == 0:
                value = value + added[at : at + 16]
            sig = jax.nn.sigmoid(value)
            act_ref[i, :, lanes] = (value * sig).astype(BF16)
            grad = cot_ref[i, :, lanes].astype(F32) * (sig * (1.0 + value * (1.0 - sig)))
            grad = grad.astype(BF16)
            gp_ref[at : at + 16] = grad
            if i == 0:
                first_ref[at : at + 16] = grad

    turned_ref[...] = dot_nt(order_ref[...], gp_ref[...]).astype(BF16)
    add_terms(turned_ref[: 2 * send_ref.shape[0]], edge, wide, terms)
    send_ref[...] = terms[...].astype(BF16)


def keep_kernel(turned_ref, edge, wide, keep_ref):
    add_terms(turned_ref[2 * keep_ref.shape[0] :], edge, wide, keep_ref)


def input_kernel(gp_ref, below_ref, w_ref, out_ref, done_ref, band):
    done_ref[...] = jnp.zeros_like(done_ref)
    for tap in range(TAPS):
        w = w_ref[tap]
        even = jnp.concatenate([blank(32, COUT), w, blank(192, COUT)], axis=0)
        odd = jnp.concatenate([blank(224, COUT), w], axis=0)
        band[tap * SPAN : (tap + 1) * SPAN] = jnp.concatenate([even, odd], axis=1)
    per_out = below_ref.shape[0]
    cells = per_out // 16
    here = gp_ref[...]
    following = below_ref[...]
    last = lax.axis_index("space") == lax.axis_size("space") - 1
    following = jnp.where(last, jnp.zeros_like(following), following)
    there = jnp.concatenate([here[per_out:], following], axis=0)
    count = gp_ref.shape[0]
    outs = count // per_out
    shape = (128, 128)
    row = iota(shape, 0)
    below = jnp.where((iota(shape, 1) == row + 1) & ((row & 15) != 15), 1.0, 0.0).astype(BF16)

    def lowered(block):
        return jnp.concatenate(
            [dot(below, block[at : at + 128]).astype(BF16) for at in range(0, count, 128)], axis=0
        )

    here_low = lowered(here)
    there_low = lowered(there)

    def term(grad, a, b):
        tap = a * 3 + b
        return dot_nt(grad, band[tap * SPAN : (tap + 1) * SPAN])

    groups = {
        (0, 0): term(here, 1, 1),
        (0, 1): term(here, 1, 2) + term(here_low, 1, 0),
        (1, 0): term(here, 2, 1) + term(there, 0, 1),
        (1, 1): term(here, 2, 2) + term(here_low, 2, 0) + term(there, 0, 2) + term(there_low, 0, 0),
    }
    shape = (32, 32)
    row = iota(shape, 0)
    weave = jnp.where(iota(shape, 1) == (row >> 1) + (row & 1) * 16, 1.0, 0.0).astype(BF16)
    for i in range(outs):
        for m in range(cells):
            at = i * per_out + m * 16
            for pd in range(2):
                parts = []
                for ph in range(2):
                    y = groups[pd, ph]
                    body = y[at : at + 16, 128:512]
                    if m + 1 < cells:
                        body = jnp.concatenate(
                            [body[:, :256], body[:, 256:] + y[at + 16 : at + 32, :128]], axis=1
                        )
                    parts.append(body.astype(BF16))
                mixed = dot(weave, jnp.concatenate(parts, axis=0)).astype(BF16)
                out_ref[2 * i + pd, :, m * BLOCK : (m + 1) * BLOCK] = mixed


def sample_bits():
    at = lax.axis_index("sample")
    return at % 2, at // (lax.axis_size("sample") // 2)


def listed(block):
    rows, lanes = block.shape
    return jnp.concatenate(
        [block[r : r + 8, t : t + 128] for r in range(0, rows, 8) for t in range(0, lanes, 128)],
        axis=0,
    )


def unlisted(tiles, rows):
    across = tiles.shape[0] // rows
    return jnp.concatenate(
        [
            jnp.concatenate(
                [tiles[(r * across + t) * 8 : (r * across + t) * 8 + 8] for t in range(across)], axis=1
            )
            for r in range(rows // 8)
        ],
        axis=0,
    )


def pair_kernel(keep_ref, got_ref, mine_ref, low_ref, high_ref):
    low, high = sample_bits()
    steps, side = low_ref.shape[:2]
    rows = keep_ref.shape[0] // steps

    def total(start, lanes):
        lanes = pl.ds(pl.multiple_of(start, 128), lanes)
        return keep_ref[:, lanes] + got_ref[:, lanes].astype(F32)

    sent = total((1 - low) * SIDE, SIDE), total((3 - high) * SIDE, SIDE)
    kept = total(low * SIDE, SIDE), total((2 + high) * SIDE, SIDE)
    last = keep_ref[:, REST:] + got_ref[:, REST:].astype(F32)
    lane = iota((8, 128), 1)
    for k in range(steps):
        at = slice(k * rows, (k + 1) * rows)
        low_ref[k] = listed(sent[0][at]).astype(BF16)
        high_ref[k] = listed(sent[1][at]).astype(BF16)
        mine_ref[k, :side] = listed(kept[0][at])
        mine_ref[k, side : 2 * side] = listed(kept[1][at])
        packed = jnp.zeros((8, 128), F32)
        for r in range(rows // 8):
            tile = last[k * rows + r * 8 : k * rows + r * 8 + 8]
            packed = packed + pltpu.roll(jnp.where(lane < LEFT, tile, 0.0), r * LEFT, 1)
        mine_ref[k, 2 * side :] = packed


def cross_kernel(mine_ref, low_ref, high_ref, *out_refs):
    side = low_ref.shape[1]
    for k, out_ref in enumerate(out_refs):
        total = jnp.concatenate(
            [
                mine_ref[k, :side] + low_ref[k].astype(F32),
                mine_ref[k, side : 2 * side] + high_ref[k].astype(F32),
                mine_ref[k, 2 * side :],
            ],
            axis=0,
        )
        out_ref[...] = total.astype(out_ref.dtype)


def depth_kernel(done_ref, own_ref, *refs):
    del done_ref
    total = own_ref[...]
    for ref in refs[:-1]:
        total = total + ref[...].astype(F32)
    refs[-1][...] = total.astype(BF16)


def store_kernel(total_ref, *refs):
    del total_ref
    count = (len(refs) - 1) // 2
    sems = refs[-1]
    copies = [pltpu.make_async_copy(refs[n], refs[count + n], sems.at[n]) for n in range(count)]
    for copy in copies:
        copy.start()
    for copy in copies:
        copy.wait()


def tree(parts):
    while len(parts) > 1:
        parts = [parts[n] + parts[n + 1] for n in range(0, len(parts), 2)]
    return parts[0]


def sample_kernel(scale, *refs):
    out_ref = refs[-1]
    width = out_ref.shape[1]
    rows = -(-width // 8) * 8
    side = rows * SIDE // 128
    parts = [ref[...].astype(F32) * scale for ref in refs[:-1]]
    half = len(parts) // 2
    here = tree([part[:side] for part in parts[0::2]])
    there = tree([part[:side] for part in parts[1::2]])
    above = tree([part[side : 2 * side] for part in parts[:half]])
    below = tree([part[side : 2 * side] for part in parts[half:]])
    packed = tree([part[2 * side :] for part in parts])
    low, high = (bit == 0 for bit in sample_bits())
    quarters = (
        jnp.where(low, here, there),
        jnp.where(low, there, here),
        jnp.where(high, above, below),
        jnp.where(high, below, above),
    )
    last = [pltpu.roll(packed, (128 - r * LEFT) % 128, 1) for r in range(rows // 8)]
    total = jnp.concatenate(
        [unlisted(quarter, rows) for quarter in quarters] + [jnp.concatenate(last, axis=0)], axis=1
    )
    total = total[:width]
    for n in range(out_ref.shape[0]):
        out_ref[n] = total[:, n * CIN : (n + 1) * CIN]


def flipped(size, bits):
    return [(i, i ^ bits) for i in range(size)]


def per_device(slabs, weight, cotangent):
    samples, planes, rows, lanes = slabs.shape
    outs = planes // 2
    space = lax.axis_size("space")
    sample = lax.axis_size("sample")
    depth = space // 2
    width = COUT // space
    high = -(-width // 8) * 8
    kept_rows = depth * high
    terms = (kept_rows, TERMS)
    side = high * SIDE // 128
    part = (2 * side + 8, 128)
    cells = lanes // BLOCK
    per_out = cells * 16
    count = outs * per_out

    in_chip = flipped(space, 1)
    onward = [(i, (i + 1) % space) for i in range(space)]
    back = [(b, a) for a, b in onward]

    x = slabs.reshape(planes, rows, lanes)
    cot = cotangent.reshape(outs, rows // 2, lanes)
    w = weight.reshape(TAPS, 3 * CIN, COUT)
    vmem = pl.BlockSpec(memory_space=pltpu.VMEM)
    hbm = pl.BlockSpec(memory_space=pltpu.HBM)
    params = pltpu.CompilerParams(vmem_limit_bytes=VMEM_LIMIT)
    shape = jax.ShapeDtypeStruct
    flops = 2 * count * TAPS * SPAN * BLOCK

    edge, split, order = pl.pallas_call(
        functools.partial(edge_kernel, width),
        out_shape=(
            shape((rows, lanes), BF16),
            shape((3 * planes * 16, planes * 32), BF16),
            shape((4 * kept_rows, 2 * COUT), BF16),
        ),
        in_specs=[hbm],
        out_specs=(vmem,) * 3,
        scratch_shapes=[pltpu.SemaphoreType.DMA(())],
        compiler_params=params,
        cost_estimate=pl.CostEstimate(flops=0, bytes_accessed=10 << 20, transcendentals=0),
        name="edge_plane",
    )(pltpu.with_memory_space_constraint(x, pltpu.HBM))
    above = lax.ppermute(edge, "space", onward)
    wide, even_band, odd_band, preact, w_in = pl.pallas_call(
        own_kernel,
        out_shape=(
            shape((count, TAPS * SPAN), BF16),
            shape((TAPS * BLOCK, COUT), BF16),
            shape((TAPS * BLOCK, COUT), BF16),
            shape((count, BLOCK), F32),
            shape(w.shape, BF16),
        ),
        in_specs=[vmem, vmem, hbm],
        out_specs=(vmem,) * 5,
        scratch_shapes=[pltpu.SemaphoreType.DMA(())],
        compiler_params=params,
        cost_estimate=pl.CostEstimate(flops=flops, bytes_accessed=12 << 20, transcendentals=0),
        name="own_planes",
    )(x, split, pltpu.with_memory_space_constraint(w, pltpu.HBM))

    act, grad, first, turned, halo, send = pl.pallas_call(
        halo_kernel,
        out_shape=(
            shape(cot.shape, BF16),
            shape((count, BLOCK), BF16),
            shape((per_out, BLOCK), BF16),
            shape((4 * kept_rows, count), BF16),
            shape((per_out, 3 * SPAN), BF16),
            shape(terms, BF16),
        ),
        in_specs=[vmem] * 7,
        out_specs=(vmem,) * 6,
        scratch_shapes=[pltpu.VMEM(terms, F32)],
        compiler_params=params,
        cost_estimate=pl.CostEstimate(
            flops=flops // 2, bytes_accessed=8 << 20, transcendentals=count * BLOCK
        ),
        name="halo_and_sent_half",
    )(above, order, wide, even_band, odd_band, preact, cot)
    got = lax.ppermute(send, "space", in_chip)
    below = lax.ppermute(first, "space", back)
    keep = pl.pallas_call(
        keep_kernel,
        out_shape=shape(terms, F32),
        in_specs=[vmem] * 3,
        out_specs=vmem,
        compiler_params=params,
        cost_estimate=pl.CostEstimate(flops=flops // 2, bytes_accessed=8 << 20, transcendentals=0),
        name="kept_half",
    )(turned, halo, wide)

    mine, low, high_lanes = pl.pallas_call(
        pair_kernel,
        out_shape=(
            shape((depth,) + part, F32),
            shape((depth, side, 128), BF16),
            shape((depth, side, 128), BF16),
        ),
        in_specs=[vmem] * 2,
        out_specs=(vmem,) * 3,
        compiler_params=params,
        name="pair_sum",
    )(keep, got)
    low = lax.ppermute(low, "sample", flipped(sample, 1))
    high_lanes = lax.ppermute(high_lanes, "sample", flipped(sample, sample // 2))
    own, *leaving = pl.pallas_call(
        cross_kernel,
        out_shape=(shape(part, F32),) + (shape(part, BF16),) * (depth - 1),
        in_specs=[vmem] * 3,
        out_specs=(vmem,) * depth,
        compiler_params=params,
        name="cross_sum",
    )(mine, low, high_lanes)
    came = [
        lax.ppermute(leaving[k - 1], "space", flipped(space, 2 * k))
        for k in [*range(depth // 2, depth), *range(1, depth // 2)]
    ]

    grad_in, done = pl.pallas_call(
        input_kernel,
        out_shape=(shape(x.shape, BF16), shape((8, 128), F32)),
        in_specs=[vmem] * 3,
        out_specs=(vmem, vmem),
        scratch_shapes=[pltpu.VMEM((TAPS * SPAN, BLOCK), BF16)],
        compiler_params=params,
        cost_estimate=pl.CostEstimate(flops=flops, bytes_accessed=8 << 20, transcendentals=0),
        name="input_grad",
    )(grad, below, w_in)

    total = pl.pallas_call(
        depth_kernel,
        out_shape=shape(part, BF16),
        in_specs=[vmem] * (depth + 1),
        out_specs=vmem,
        compiler_params=params,
        name="depth_sum",
    )(done, own, *came)
    act, grad_in = pl.pallas_call(
        store_kernel,
        out_shape=(shape(cot.shape, BF16), shape(x.shape, BF16)),
        in_specs=[vmem] * 3,
        out_specs=(hbm, hbm),
        scratch_shapes=[pltpu.SemaphoreType.DMA((2,))],
        compiler_params=params,
        name="store",
    )(total, act, grad_in)
    others = [lax.ppermute(total, "sample", flipped(sample, j)) for j in range(1, sample)]
    kernel_grad = pl.pallas_call(
        functools.partial(sample_kernel, 1.0 / (samples * sample)),
        out_shape=shape((TAPS * 3, width, CIN), F32),
        in_specs=[vmem] * sample,
        out_specs=vmem,
        compiler_params=params,
        name="sample_sum",
    )(total, *others)
    kernel_grad = jnp.transpose(kernel_grad, (0, 2, 1)).reshape(3, 3, 3, CIN, width)
    return act.reshape(cotangent.shape), grad_in.reshape(slabs.shape), kernel_grad


def solution(mesh):
    placed = (P("sample", "space", None, None), P(), P("sample", "space", None, None))
    return jax.shard_map(
        per_device,
        mesh=mesh,
        in_specs=placed,
        out_specs=(
            P("sample", "space", None, None),
            P("sample", "space", None, None),
            P(None, None, None, None, "space"),
        ),
        check_vma=False,
    )
```

```python
import functools

import jax
import jax.numpy as jnp
from jax import lax
from jax.experimental import pallas as pl
from jax.experimental.pallas import tpu as pltpu
from jax.sharding import PartitionSpec as P

CIN = 96
COUT = 192
BLOCK = 384
SPAN = 512
TAPS = 9
SIDE = 640
REST = 4 * SIDE
TERMS = REST + 128
LEFT = TAPS * 3 * CIN - REST
F32 = jnp.float32
BF16 = jnp.bfloat16
VMEM_LIMIT = 12 * 1024 * 1024


def iota(shape, axis):
    return lax.broadcasted_iota(jnp.int32, shape, axis)


def row_split(planes):
    shape = (3 * planes * 16, planes * 32)
    row = iota(shape, 0)
    col = iota(shape, 1)
    j = row & 15
    plane = (row >> 4) & (planes - 1)
    b = jnp.where(row >= planes * 32, 2, jnp.where(row >= planes * 16, 1, 0))
    hit = (col == plane * 32 + 2 * j + b - 1) & ((j + b) > 0)
    return jnp.where(hit, 1.0, 0.0).astype(BF16)


def blank(rows, lanes):
    return jnp.zeros((rows, lanes), BF16)


def dot(lhs, rhs):
    return jnp.dot(lhs, rhs, preferred_element_type=F32)


def dot_nt(lhs, rhs):
    return lax.dot_general(lhs, rhs, (((1,), (1,)), ((), ())), preferred_element_type=F32)


def put(wide, per_out, cells, i, m, tap, piece):
    at = i * per_out + m * 16
    wide[at : at + 16, tap * SPAN + 128 : tap * SPAN + 512] = piece
    if m + 1 < cells:
        wide[at + 16 : at + 32, tap * SPAN : tap * SPAN + 128] = piece[:, 256:]
    if m == 0:
        wide[at : at + 16, tap * SPAN : tap * SPAN + 128] = jnp.zeros((16, 128), BF16)


def edge_kernel(width, x_hbm, edge_ref, split_ref, order_ref, sem):
    copy = pltpu.make_async_copy(x_hbm.at[x_hbm.shape[0] - 1], edge_ref, sem)
    copy.start()
    split_ref[...] = row_split(x_hbm.shape[0])
    at = lax.axis_index("space")
    core = at % 2
    chip = at // 2
    steps = lax.axis_size("space") // 2
    shape = order_ref.shape
    rows = shape[0] // 4
    high = rows // steps
    inner = iota(shape, 0)
    kept = inner >= 2 * rows
    inner = inner - jnp.where(kept, 2 * rows, 0)
    odd = inner >= rows
    inner = inner - jnp.where(odd, rows, 0)
    source = jnp.where(kept, core, 1 - core) * width + jnp.where(odd, COUT, 0)
    for k in range(steps):
        channel = inner - k * high
        inside = (channel >= 0) & (channel < width)
        source = source + jnp.where(inside, channel + (chip ^ k) * 2 * width, 0)
        if high != width:
            source = jnp.where((channel >= width) & (channel < high), -1, source)
    order_ref[...] = jnp.where(iota(shape, 1) == source, 1.0, 0.0).astype(BF16)
    copy.wait()


def by_parity(wide, even_band, odd_band, taps):
    sides = []
    for start, band in ((0, even_band), (SPAN - BLOCK, odd_band)):
        windows = [wide[:, tap * SPAN + start : tap * SPAN + start + BLOCK] for tap in range(taps)]
        sides.append(dot(jnp.concatenate(windows, axis=1), band[: taps * BLOCK]))
    return sides


def own_kernel(x_ref, split_ref, w_hbm, wide, even_band, odd_band, preact, w_ref, sem):
    planes = x_ref.shape[0]
    outs = planes // 2
    cells = x_ref.shape[2] // BLOCK
    per_out = cells * 16
    copy = pltpu.make_async_copy(w_hbm, w_ref, sem)
    copy.start()
    split = split_ref[...]
    wide[0:per_out, 0 : 3 * SPAN] = jnp.zeros((per_out, 3 * SPAN), BF16)
    x = x_ref[...].reshape(planes * 32, x_ref.shape[2])
    for m in range(cells):
        rows = dot(split, x[:, m * BLOCK : (m + 1) * BLOCK]).astype(BF16)
        for b in range(3):
            for p in range(planes):
                piece = rows[(b * planes + p) * 16 : (b * planes + p + 1) * 16]
                if p % 2 == 0:
                    put(wide, per_out, cells, p // 2, m, 3 + b, piece)
                else:
                    put(wide, per_out, cells, p // 2, m, 6 + b, piece)
                    if p // 2 + 1 < outs:
                        put(wide, per_out, cells, p // 2 + 1, m, b, piece)
    copy.wait()
    for tap in range(TAPS):
        at = tap * BLOCK
        even_band[at : at + 32] = blank(32, COUT)
        even_band[at + 32 : at + 320] = w_ref[tap]
        even_band[at + 320 : at + BLOCK] = blank(64, COUT)
        odd_band[at : at + 96] = blank(96, COUT)
        odd_band[at + 96 : at + BLOCK] = w_ref[tap]
    even, odd = by_parity(wide, even_band, odd_band, TAPS)
    preact[:, :COUT] = even
    preact[:, COUT:] = odd


def add_terms(turned, edge, wide, terms):
    rows = terms.shape[0]
    per_out = edge.shape[0]
    terms[...] = jnp.zeros_like(terms)
    lane = iota((rows, SPAN), 1)
    even_lanes = (lane >= 32) & (lane < 320)
    odd_lanes = lane >= 224
    for tap in range(TAPS):
        lanes = slice(tap * SPAN, (tap + 1) * SPAN)
        if tap < 3:
            cols = jnp.concatenate([edge[:, lanes], wide[per_out:, lanes]], axis=0)
        else:
            cols = wide[:, lanes]
        both = dot(turned, cols)
        base = tap * 288 // 128 * 128
        shift = tap * 288 - base
        even = jnp.where(even_lanes, both[:rows], 0.0)
        odd = jnp.where(odd_lanes, both[rows:], 0.0)
        even = pltpu.roll(even, (shift - 32) % SPAN, 1)
        odd = pltpu.roll(odd, (shift - 224) % SPAN, 1)
        terms[:, base : base + BLOCK] += (even + odd)[:, :BLOCK]


def halo_kernel(
    above_ref, order_ref, wide, even_band, odd_band, pre_ref, cot_ref,
    act_ref, gp_ref, first_ref, turned_ref, edge, send_ref, terms,
):
    outs = cot_ref.shape[0]
    cells = cot_ref.shape[2] // BLOCK
    per_out = cells * 16
    top = lax.axis_index("space") == 0
    split_one = row_split(1)
    for m in range(cells):
        lanes = slice(m * BLOCK, (m + 1) * BLOCK)
        plane = above_ref[:, lanes]
        plane = jnp.where(top, jnp.zeros_like(plane), plane)
        above = dot(split_one, plane).astype(BF16)
        for b in range(3):
            put(edge, per_out, cells, 0, m, b, above[b * 16 : b * 16 + 16])
    added = jnp.concatenate(by_parity(edge, even_band, odd_band, 3), axis=1)
    for i in range(outs):
        for m in range(cells):
            lanes = slice(m * BLOCK, (m + 1) * BLOCK)
            at = i * per_out + m * 16
            value = pre_ref[at : at + 16]
            if i == 0:
                value = value + added[at : at + 16]
            sig = jax.nn.sigmoid(value)
            act_ref[i, :, lanes] = (value * sig).astype(BF16)
            grad = cot_ref[i, :, lanes].astype(F32) * (sig * (1.0 + value * (1.0 - sig)))
            grad = grad.astype(BF16)
            gp_ref[at : at + 16] = grad
            if i == 0:
                first_ref[at : at + 16] = grad

    turned_ref[...] = dot_nt(order_ref[...], gp_ref[...]).astype(BF16)
    add_terms(turned_ref[: 2 * send_ref.shape[0]], edge, wide, terms)
    send_ref[...] = terms[...].astype(BF16)


def keep_kernel(turned_ref, edge, wide, keep_ref):
    add_terms(turned_ref[2 * keep_ref.shape[0] :], edge, wide, keep_ref)


def input_kernel(gp_ref, below_ref, w_ref, out_ref, done_ref, band):
    done_ref[...] = jnp.zeros_like(done_ref)
    for tap in range(TAPS):
        w = w_ref[tap]
        even = jnp.concatenate([blank(32, COUT), w, blank(192, COUT)], axis=0)
        odd = jnp.concatenate([blank(224, COUT), w], axis=0)
        band[tap * SPAN : (tap + 1) * SPAN] = jnp.concatenate([even, odd], axis=1)
    per_out = below_ref.shape[0]
    cells = per_out // 16
    here = gp_ref[...]
    following = below_ref[...]
    last = lax.axis_index("space") == lax.axis_size("space") - 1
    following = jnp.where(last, jnp.zeros_like(following), following)
    there = jnp.concatenate([here[per_out:], following], axis=0)
    count = gp_ref.shape[0]
    outs = count // per_out
    shape = (128, 128)
    row = iota(shape, 0)
    below = jnp.where((iota(shape, 1) == row + 1) & ((row & 15) != 15), 1.0, 0.0).astype(BF16)

    def lowered(block):
        return jnp.concatenate(
            [dot(below, block[at : at + 128]).astype(BF16) for at in range(0, count, 128)], axis=0
        )

    here_low = lowered(here)
    there_low = lowered(there)

    def term(grad, a, b):
        tap = a * 3 + b
        return dot_nt(grad, band[tap * SPAN : (tap + 1) * SPAN])

    groups = {
        (0, 0): term(here, 1, 1),
        (0, 1): term(here, 1, 2) + term(here_low, 1, 0),
        (1, 0): term(here, 2, 1) + term(there, 0, 1),
        (1, 1): term(here, 2, 2) + term(here_low, 2, 0) + term(there, 0, 2) + term(there_low, 0, 0),
    }
    shape = (32, 32)
    row = iota(shape, 0)
    weave = jnp.where(iota(shape, 1) == (row >> 1) + (row & 1) * 16, 1.0, 0.0).astype(BF16)
    for i in range(outs):
        for m in range(cells):
            at = i * per_out + m * 16
            for pd in range(2):
                parts = []
                for ph in range(2):
                    y = groups[pd, ph]
                    body = y[at : at + 16, 128:512]
                    if m + 1 < cells:
                        body = jnp.concatenate(
                            [body[:, :256], body[:, 256:] + y[at + 16 : at + 32, :128]], axis=1
                        )
                    parts.append(body.astype(BF16))
                mixed = dot(weave, jnp.concatenate(parts, axis=0)).astype(BF16)
                out_ref[2 * i + pd, :, m * BLOCK : (m + 1) * BLOCK] = mixed


def sample_bits():
    at = lax.axis_index("sample")
    return at % 2, at // (lax.axis_size("sample") // 2)


def listed(block):
    rows, lanes = block.shape
    return jnp.concatenate(
        [block[r : r + 8, t : t + 128] for r in range(0, rows, 8) for t in range(0, lanes, 128)],
        axis=0,
    )


def unlisted(tiles, rows):
    across = tiles.shape[0] // rows
    return jnp.concatenate(
        [
            jnp.concatenate(
                [tiles[(r * across + t) * 8 : (r * across + t) * 8 + 8] for t in range(across)], axis=1
            )
            for r in range(rows // 8)
        ],
        axis=0,
    )


def pair_kernel(keep_ref, got_ref, *refs):
    low, high = sample_bits()
    half, side = refs[1].shape[:2]
    rows = keep_ref.shape[0] // (2 * half)

    def total(start, lanes):
        lanes = pl.ds(pl.multiple_of(start, 128), lanes)
        return keep_ref[:, lanes] + got_ref[:, lanes].astype(F32)

    sent = total((1 - low) * SIDE, SIDE), total((3 - high) * SIDE, SIDE)
    kept = total(low * SIDE, SIDE), total((2 + high) * SIDE, SIDE)
    last = keep_ref[:, REST:] + got_ref[:, REST:].astype(F32)
    lane = iota((8, 128), 1)
    for k in range(2 * half):
        mine_ref, low_ref, high_ref = refs[:3] if k >= half else refs[3:]
        at = slice(k * rows, (k + 1) * rows)
        to = k % half
        low_ref[to] = listed(sent[0][at]).astype(BF16)
        high_ref[to] = listed(sent[1][at]).astype(BF16)
        mine_ref[to, :side] = listed(kept[0][at])
        mine_ref[to, side : 2 * side] = listed(kept[1][at])
        packed = jnp.zeros((8, 128), F32)
        for r in range(rows // 8):
            tile = last[k * rows + r * 8 : k * rows + r * 8 + 8]
            packed = packed + pltpu.roll(jnp.where(lane < LEFT, tile, 0.0), r * LEFT, 1)
        mine_ref[to, 2 * side :] = packed


def cross_kernel(mine_ref, low_ref, high_ref, *out_refs):
    side = low_ref.shape[1]
    for k, out_ref in enumerate(out_refs):
        total = jnp.concatenate(
            [
                mine_ref[k, :side] + low_ref[k].astype(F32),
                mine_ref[k, side : 2 * side] + high_ref[k].astype(F32),
                mine_ref[k, 2 * side :],
            ],
            axis=0,
        )
        out_ref[...] = total.astype(out_ref.dtype)


def later_cross_kernel(early, *refs):
    cross_kernel(*refs[early:])


def depth_kernel(done_ref, own_ref, *refs):
    del done_ref
    total = own_ref[...]
    for ref in refs[:-1]:
        total = total + ref[...].astype(F32)
    refs[-1][...] = total.astype(BF16)


def store_kernel(total_ref, *refs):
    del total_ref
    count = (len(refs) - 1) // 2
    sems = refs[-1]
    copies = [pltpu.make_async_copy(refs[n], refs[count + n], sems.at[n]) for n in range(count)]
    for copy in copies:
        copy.start()
    for copy in copies:
        copy.wait()


def tree(parts):
    while len(parts) > 1:
        parts = [parts[n] + parts[n + 1] for n in range(0, len(parts), 2)]
    return parts[0]


def sample_kernel(scale, *refs):
    out_ref = refs[-1]
    width = out_ref.shape[1]
    rows = -(-width // 8) * 8
    side = rows * SIDE // 128
    parts = [ref[...].astype(F32) * scale for ref in refs[:-1]]
    half = len(parts) // 2
    here = tree([part[:side] for part in parts[0::2]])
    there = tree([part[:side] for part in parts[1::2]])
    above = tree([part[side : 2 * side] for part in parts[:half]])
    below = tree([part[side : 2 * side] for part in parts[half:]])
    packed = tree([part[2 * side :] for part in parts])
    low, high = (bit == 0 for bit in sample_bits())
    quarters = (
        jnp.where(low, here, there),
        jnp.where(low, there, here),
        jnp.where(high, above, below),
        jnp.where(high, below, above),
    )
    last = [pltpu.roll(packed, (128 - r * LEFT) % 128, 1) for r in range(rows // 8)]
    total = jnp.concatenate(
        [unlisted(quarter, rows) for quarter in quarters] + [jnp.concatenate(last, axis=0)], axis=1
    )
    total = total[:width]
    for n in range(out_ref.shape[0]):
        out_ref[n] = total[:, n * CIN : (n + 1) * CIN]


def flipped(size, bits):
    return [(i, i ^ bits) for i in range(size)]


def per_device(slabs, weight, cotangent):
    samples, planes, rows, lanes = slabs.shape
    outs = planes // 2
    space = lax.axis_size("space")
    sample = lax.axis_size("sample")
    depth = space // 2
    width = COUT // space
    high = -(-width // 8) * 8
    kept_rows = depth * high
    terms = (kept_rows, TERMS)
    side = high * SIDE // 128
    part = (2 * side + 8, 128)
    cells = lanes // BLOCK
    per_out = cells * 16
    count = outs * per_out

    in_chip = flipped(space, 1)
    onward = [(i, (i + 1) % space) for i in range(space)]
    back = [(b, a) for a, b in onward]

    x = slabs.reshape(planes, rows, lanes)
    cot = cotangent.reshape(outs, rows // 2, lanes)
    w = weight.reshape(TAPS, 3 * CIN, COUT)
    vmem = pl.BlockSpec(memory_space=pltpu.VMEM)
    hbm = pl.BlockSpec(memory_space=pltpu.HBM)
    params = pltpu.CompilerParams(vmem_limit_bytes=VMEM_LIMIT)
    shape = jax.ShapeDtypeStruct
    flops = 2 * count * TAPS * SPAN * BLOCK

    edge, split, order = pl.pallas_call(
        functools.partial(edge_kernel, width),
        out_shape=(
            shape((rows, lanes), BF16),
            shape((3 * planes * 16, planes * 32), BF16),
            shape((4 * kept_rows, 2 * COUT), BF16),
        ),
        in_specs=[hbm],
        out_specs=(vmem,) * 3,
        scratch_shapes=[pltpu.SemaphoreType.DMA(())],
        compiler_params=params,
        cost_estimate=pl.CostEstimate(flops=0, bytes_accessed=10 << 20, transcendentals=0),
        name="edge_plane",
    )(pltpu.with_memory_space_constraint(x, pltpu.HBM))
    above = lax.ppermute(edge, "space", onward)
    wide, even_band, odd_band, preact, w_in = pl.pallas_call(
        own_kernel,
        out_shape=(
            shape((count, TAPS * SPAN), BF16),
            shape((TAPS * BLOCK, COUT), BF16),
            shape((TAPS * BLOCK, COUT), BF16),
            shape((count, BLOCK), F32),
            shape(w.shape, BF16),
        ),
        in_specs=[vmem, vmem, hbm],
        out_specs=(vmem,) * 5,
        scratch_shapes=[pltpu.SemaphoreType.DMA(())],
        compiler_params=params,
        cost_estimate=pl.CostEstimate(flops=flops, bytes_accessed=12 << 20, transcendentals=0),
        name="own_planes",
    )(x, split, pltpu.with_memory_space_constraint(w, pltpu.HBM))

    act, grad, first, turned, halo, send = pl.pallas_call(
        halo_kernel,
        out_shape=(
            shape(cot.shape, BF16),
            shape((count, BLOCK), BF16),
            shape((per_out, BLOCK), BF16),
            shape((4 * kept_rows, count), BF16),
            shape((per_out, 3 * SPAN), BF16),
            shape(terms, BF16),
        ),
        in_specs=[vmem] * 7,
        out_specs=(vmem,) * 6,
        scratch_shapes=[pltpu.VMEM(terms, F32)],
        compiler_params=params,
        cost_estimate=pl.CostEstimate(
            flops=flops // 2, bytes_accessed=8 << 20, transcendentals=count * BLOCK
        ),
        name="halo_and_sent_half",
    )(above, order, wide, even_band, odd_band, preact, cot)
    got = lax.ppermute(send, "space", in_chip)
    below = lax.ppermute(first, "space", back)
    keep = pl.pallas_call(
        keep_kernel,
        out_shape=shape(terms, F32),
        in_specs=[vmem] * 3,
        out_specs=vmem,
        compiler_params=params,
        cost_estimate=pl.CostEstimate(flops=flops // 2, bytes_accessed=8 << 20, transcendentals=0),
        name="kept_half",
    )(turned, halo, wide)

    half = depth // 2
    batch = (
        shape((half,) + part, F32),
        shape((half, side, 128), BF16),
        shape((half, side, 128), BF16),
    )
    early_mine, early_low, early_high, later_mine, later_low, later_high = pl.pallas_call(
        pair_kernel,
        out_shape=batch * 2,
        in_specs=[vmem] * 2,
        out_specs=(vmem,) * 6,
        compiler_params=params,
        name="pair_sum",
    )(keep, got)

    def crossed(low_half, high_half):
        return (
            lax.ppermute(low_half, "sample", flipped(sample, 1)),
            lax.ppermute(high_half, "sample", flipped(sample, sample // 2)),
        )

    early = crossed(early_low, early_high)
    later = crossed(later_low, later_high)
    leaving = pl.pallas_call(
        cross_kernel,
        out_shape=(shape(part, BF16),) * half,
        in_specs=[vmem] * 3,
        out_specs=(vmem,) * half,
        compiler_params=params,
        name="early_cross_sum",
    )(early_mine, *early)
    came = [
        lax.ppermute(leaving[k - half], "space", flipped(space, 2 * k)) for k in range(half, depth)
    ]
    own, *leaving = pl.pallas_call(
        functools.partial(later_cross_kernel, half),
        out_shape=(shape(part, F32),) + (shape(part, BF16),) * (half - 1),
        in_specs=[vmem] * (half + 3),
        out_specs=(vmem,) * half,
        compiler_params=params,
        name="later_cross_sum",
    )(*leaving, later_mine, *later)
    came += [lax.ppermute(leaving[k - 1], "space", flipped(space, 2 * k)) for k in range(1, half)]

    grad_in, done = pl.pallas_call(
        input_kernel,
        out_shape=(shape(x.shape, BF16), shape((8, 128), F32)),
        in_specs=[vmem] * 3,
        out_specs=(vmem, vmem),
        scratch_shapes=[pltpu.VMEM((TAPS * SPAN, BLOCK), BF16)],
        compiler_params=params,
        cost_estimate=pl.CostEstimate(flops=flops, bytes_accessed=8 << 20, transcendentals=0),
        name="input_grad",
    )(grad, below, w_in)

    total = pl.pallas_call(
        depth_kernel,
        out_shape=shape(part, BF16),
        in_specs=[vmem] * (depth + 1),
        out_specs=vmem,
        compiler_params=params,
        name="depth_sum",
    )(done, own, *came)
    act, grad_in = pl.pallas_call(
        store_kernel,
        out_shape=(shape(cot.shape, BF16), shape(x.shape, BF16)),
        in_specs=[vmem] * 3,
        out_specs=(hbm, hbm),
        scratch_shapes=[pltpu.SemaphoreType.DMA((2,))],
        compiler_params=params,
        name="store",
    )(total, act, grad_in)
    others = [lax.ppermute(total, "sample", flipped(sample, j)) for j in range(1, sample)]
    kernel_grad = pl.pallas_call(
        functools.partial(sample_kernel, 1.0 / (samples * sample)),
        out_shape=shape((TAPS * 3, width, CIN), F32),
        in_specs=[vmem] * sample,
        out_specs=vmem,
        compiler_params=params,
        name="sample_sum",
    )(total, *others)
    kernel_grad = jnp.transpose(kernel_grad, (0, 2, 1)).reshape(3, 3, 3, CIN, width)
    return act.reshape(cotangent.shape), grad_in.reshape(slabs.shape), kernel_grad


def solution(mesh):
    placed = (P("sample", "space", None, None), P(), P("sample", "space", None, None))
    return jax.shard_map(
        per_device,
        mesh=mesh,
        in_specs=placed,
        out_specs=(
            P("sample", "space", None, None),
            P("sample", "space", None, None),
            P(None, None, None, None, "space"),
        ),
        check_vma=False,
    )
```

```python
import functools

import jax
import jax.numpy as jnp
from jax import lax
from jax.experimental import pallas as pl
from jax.experimental.pallas import tpu as pltpu
from jax.sharding import PartitionSpec as P

CIN = 96
COUT = 192
BLOCK = 384
SPAN = 512
TAPS = 9
SIDE = 640
REST = 4 * SIDE
TERMS = REST + 128
LEFT = TAPS * 3 * CIN - REST
F32 = jnp.float32
BF16 = jnp.bfloat16
VMEM_LIMIT = 12 * 1024 * 1024


def iota(shape, axis):
    return lax.broadcasted_iota(jnp.int32, shape, axis)


def row_split(planes):
    shape = (3 * planes * 16, planes * 32)
    row = iota(shape, 0)
    col = iota(shape, 1)
    j = row & 15
    plane = (row >> 4) & (planes - 1)
    b = jnp.where(row >= planes * 32, 2, jnp.where(row >= planes * 16, 1, 0))
    hit = (col == plane * 32 + 2 * j + b - 1) & ((j + b) > 0)
    return jnp.where(hit, 1.0, 0.0).astype(BF16)


def blank(rows, lanes):
    return jnp.zeros((rows, lanes), BF16)


def dot(lhs, rhs):
    return jnp.dot(lhs, rhs, preferred_element_type=F32)


def dot_nt(lhs, rhs):
    return lax.dot_general(lhs, rhs, (((1,), (1,)), ((), ())), preferred_element_type=F32)


def put(wide, per_out, cells, i, m, tap, piece):
    at = i * per_out + m * 16
    wide[at : at + 16, tap * SPAN + 128 : tap * SPAN + 512] = piece
    if m + 1 < cells:
        wide[at + 16 : at + 32, tap * SPAN : tap * SPAN + 128] = piece[:, 256:]
    if m == 0:
        wide[at : at + 16, tap * SPAN : tap * SPAN + 128] = jnp.zeros((16, 128), BF16)


def edge_kernel(width, x_hbm, edge_ref, split_ref, order_ref, sem):
    copy = pltpu.make_async_copy(x_hbm.at[x_hbm.shape[0] - 1], edge_ref, sem)
    copy.start()
    split_ref[...] = row_split(x_hbm.shape[0])
    at = lax.axis_index("space")
    core = at % 2
    chip = at // 2
    steps = lax.axis_size("space") // 2
    shape = order_ref.shape
    rows = shape[0] // 4
    high = rows // steps
    inner = iota(shape, 0)
    kept = inner >= 2 * rows
    inner = inner - jnp.where(kept, 2 * rows, 0)
    odd = inner >= rows
    inner = inner - jnp.where(odd, rows, 0)
    source = jnp.where(kept, core, 1 - core) * width + jnp.where(odd, COUT, 0)
    for k in range(steps):
        channel = inner - k * high
        inside = (channel >= 0) & (channel < width)
        source = source + jnp.where(inside, channel + (chip ^ k) * 2 * width, 0)
        if high != width:
            source = jnp.where((channel >= width) & (channel < high), -1, source)
    order_ref[...] = jnp.where(iota(shape, 1) == source, 1.0, 0.0).astype(BF16)
    copy.wait()


def by_parity(wide, even_band, odd_band, taps):
    sides = []
    for start, band in ((0, even_band), (SPAN - BLOCK, odd_band)):
        windows = [wide[:, tap * SPAN + start : tap * SPAN + start + BLOCK] for tap in range(taps)]
        sides.append(dot(jnp.concatenate(windows, axis=1), band[: taps * BLOCK]))
    return sides


def own_kernel(x_ref, split_ref, w_hbm, wide, even_band, odd_band, preact, w_ref, sem):
    planes = x_ref.shape[0]
    outs = planes // 2
    cells = x_ref.shape[2] // BLOCK
    per_out = cells * 16
    copy = pltpu.make_async_copy(w_hbm, w_ref, sem)
    copy.start()
    split = split_ref[...]
    wide[0:per_out, 0 : 3 * SPAN] = jnp.zeros((per_out, 3 * SPAN), BF16)
    x = x_ref[...].reshape(planes * 32, x_ref.shape[2])
    for m in range(cells):
        rows = dot(split, x[:, m * BLOCK : (m + 1) * BLOCK]).astype(BF16)
        for b in range(3):
            for p in range(planes):
                piece = rows[(b * planes + p) * 16 : (b * planes + p + 1) * 16]
                if p % 2 == 0:
                    put(wide, per_out, cells, p // 2, m, 3 + b, piece)
                else:
                    put(wide, per_out, cells, p // 2, m, 6 + b, piece)
                    if p // 2 + 1 < outs:
                        put(wide, per_out, cells, p // 2 + 1, m, b, piece)
    copy.wait()
    for tap in range(TAPS):
        at = tap * BLOCK
        even_band[at : at + 32] = blank(32, COUT)
        even_band[at + 32 : at + 320] = w_ref[tap]
        even_band[at + 320 : at + BLOCK] = blank(64, COUT)
        odd_band[at : at + 96] = blank(96, COUT)
        odd_band[at + 96 : at + BLOCK] = w_ref[tap]
    even, odd = by_parity(wide, even_band, odd_band, TAPS)
    preact[:, :COUT] = even
    preact[:, COUT:] = odd


def add_terms(turned, edge, wide, terms):
    rows = terms.shape[0]
    per_out = edge.shape[0]
    terms[...] = jnp.zeros_like(terms)
    lane = iota((rows, SPAN), 1)
    even_lanes = (lane >= 32) & (lane < 320)
    odd_lanes = lane >= 224
    for tap in range(TAPS):
        lanes = slice(tap * SPAN, (tap + 1) * SPAN)
        if tap < 3:
            cols = jnp.concatenate([edge[:, lanes], wide[per_out:, lanes]], axis=0)
        else:
            cols = wide[:, lanes]
        both = dot(turned, cols)
        base = tap * 288 // 128 * 128
        shift = tap * 288 - base
        even = jnp.where(even_lanes, both[:rows], 0.0)
        odd = jnp.where(odd_lanes, both[rows:], 0.0)
        even = pltpu.roll(even, (shift - 32) % SPAN, 1)
        odd = pltpu.roll(odd, (shift - 224) % SPAN, 1)
        terms[:, base : base + BLOCK] += (even + odd)[:, :BLOCK]


def halo_kernel(
    above_ref, order_ref, wide, even_band, odd_band, pre_ref, cot_ref,
    act_ref, gp_ref, first_ref, turned_ref, edge, send_ref, terms,
):
    outs = cot_ref.shape[0]
    cells = cot_ref.shape[2] // BLOCK
    per_out = cells * 16
    top = lax.axis_index("space") == 0
    split_one = row_split(1)
    for m in range(cells):
        lanes = slice(m * BLOCK, (m + 1) * BLOCK)
        plane = above_ref[:, lanes]
        plane = jnp.where(top, jnp.zeros_like(plane), plane)
        above = dot(split_one, plane).astype(BF16)
        for b in range(3):
            put(edge, per_out, cells, 0, m, b, above[b * 16 : b * 16 + 16])
    added = jnp.concatenate(by_parity(edge, even_band, odd_band, 3), axis=1)
    for i in range(outs):
        for m in range(cells):
            lanes = slice(m * BLOCK, (m + 1) * BLOCK)
            at = i * per_out + m * 16
            value = pre_ref[at : at + 16]
            if i == 0:
                value = value + added[at : at + 16]
            sig = jax.nn.sigmoid(value)
            act_ref[i, :, lanes] = (value * sig).astype(BF16)
            grad = cot_ref[i, :, lanes].astype(F32) * (sig * (1.0 + value * (1.0 - sig)))
            grad = grad.astype(BF16)
            gp_ref[at : at + 16] = grad
            if i == 0:
                first_ref[at : at + 16] = grad

    turned_ref[...] = dot_nt(order_ref[...], gp_ref[...]).astype(BF16)
    add_terms(turned_ref[: 2 * send_ref.shape[0]], edge, wide, terms)
    send_ref[...] = terms[...].astype(BF16)


def keep_kernel(turned_ref, edge, wide, keep_ref):
    add_terms(turned_ref[2 * keep_ref.shape[0] :], edge, wide, keep_ref)


def input_kernel(gp_ref, below_ref, w_ref, out_ref, done_ref, band):
    done_ref[...] = jnp.zeros_like(done_ref)
    for tap in range(TAPS):
        w = w_ref[tap]
        even = jnp.concatenate([blank(32, COUT), w, blank(192, COUT)], axis=0)
        odd = jnp.concatenate([blank(224, COUT), w], axis=0)
        band[tap * SPAN : (tap + 1) * SPAN] = jnp.concatenate([even, odd], axis=1)
    per_out = below_ref.shape[0]
    cells = per_out // 16
    here = gp_ref[...]
    following = below_ref[...]
    last = lax.axis_index("space") == lax.axis_size("space") - 1
    following = jnp.where(last, jnp.zeros_like(following), following)
    there = jnp.concatenate([here[per_out:], following], axis=0)
    count = gp_ref.shape[0]
    outs = count // per_out
    shape = (128, 128)
    row = iota(shape, 0)
    below = jnp.where((iota(shape, 1) == row + 1) & ((row & 15) != 15), 1.0, 0.0).astype(BF16)

    def lowered(block):
        return jnp.concatenate(
            [dot(below, block[at : at + 128]).astype(BF16) for at in range(0, count, 128)], axis=0
        )

    here_low = lowered(here)
    there_low = lowered(there)

    def term(grad, a, b):
        tap = a * 3 + b
        return dot_nt(grad, band[tap * SPAN : (tap + 1) * SPAN])

    groups = {
        (0, 0): term(here, 1, 1),
        (0, 1): term(here, 1, 2) + term(here_low, 1, 0),
        (1, 0): term(here, 2, 1) + term(there, 0, 1),
        (1, 1): term(here, 2, 2) + term(here_low, 2, 0) + term(there, 0, 2) + term(there_low, 0, 0),
    }
    shape = (32, 32)
    row = iota(shape, 0)
    weave = jnp.where(iota(shape, 1) == (row >> 1) + (row & 1) * 16, 1.0, 0.0).astype(BF16)
    for i in range(outs):
        for m in range(cells):
            at = i * per_out + m * 16
            for pd in range(2):
                parts = []
                for ph in range(2):
                    y = groups[pd, ph]
                    body = y[at : at + 16, 128:512]
                    if m + 1 < cells:
                        body = jnp.concatenate(
                            [body[:, :256], body[:, 256:] + y[at + 16 : at + 32, :128]], axis=1
                        )
                    parts.append(body.astype(BF16))
                mixed = dot(weave, jnp.concatenate(parts, axis=0)).astype(BF16)
                out_ref[2 * i + pd, :, m * BLOCK : (m + 1) * BLOCK] = mixed


def sample_bits():
    at = lax.axis_index("sample")
    return at % 2, at // (lax.axis_size("sample") // 2)


def listed(block):
    rows, lanes = block.shape
    return jnp.concatenate(
        [block[r : r + 8, t : t + 128] for r in range(0, rows, 8) for t in range(0, lanes, 128)],
        axis=0,
    )


def unlisted(tiles, rows):
    across = tiles.shape[0] // rows
    return jnp.concatenate(
        [
            jnp.concatenate(
                [tiles[(r * across + t) * 8 : (r * across + t) * 8 + 8] for t in range(across)], axis=1
            )
            for r in range(rows // 8)
        ],
        axis=0,
    )


def pair_kernel(keep_ref, got_ref, first_ref, passed_ref, *refs):
    passed_ref[...] = first_ref[...]
    low, high = sample_bits()
    half, side = refs[1].shape[:2]
    rows = keep_ref.shape[0] // (2 * half)

    def total(start, lanes):
        lanes = pl.ds(pl.multiple_of(start, 128), lanes)
        return keep_ref[:, lanes] + got_ref[:, lanes].astype(F32)

    sent = total((1 - low) * SIDE, SIDE), total((3 - high) * SIDE, SIDE)
    kept = total(low * SIDE, SIDE), total((2 + high) * SIDE, SIDE)
    last = keep_ref[:, REST:] + got_ref[:, REST:].astype(F32)
    lane = iota((8, 128), 1)
    for k in range(2 * half):
        mine_ref, low_ref, high_ref = refs[:3] if k >= half else refs[3:]
        at = slice(k * rows, (k + 1) * rows)
        to = k % half
        low_ref[to] = listed(sent[0][at]).astype(BF16)
        high_ref[to] = listed(sent[1][at]).astype(BF16)
        mine_ref[to, :side] = listed(kept[0][at])
        mine_ref[to, side : 2 * side] = listed(kept[1][at])
        packed = jnp.zeros((8, 128), F32)
        for r in range(rows // 8):
            tile = last[k * rows + r * 8 : k * rows + r * 8 + 8]
            packed = packed + pltpu.roll(jnp.where(lane < LEFT, tile, 0.0), r * LEFT, 1)
        mine_ref[to, 2 * side :] = packed


def cross_kernel(mine_ref, low_ref, high_ref, *out_refs):
    side = low_ref.shape[1]
    for k, out_ref in enumerate(out_refs):
        total = jnp.concatenate(
            [
                mine_ref[k, :side] + low_ref[k].astype(F32),
                mine_ref[k, side : 2 * side] + high_ref[k].astype(F32),
                mine_ref[k, 2 * side :],
            ],
            axis=0,
        )
        out_ref[...] = total.astype(out_ref.dtype)


def later_cross_kernel(early, *refs):
    cross_kernel(*refs[early:])


def depth_kernel(done_ref, own_ref, *refs):
    del done_ref
    total = own_ref[...]
    for ref in refs[:-1]:
        total = total + ref[...].astype(F32)
    refs[-1][...] = total.astype(BF16)


def store_kernel(total_ref, *refs):
    del total_ref
    count = (len(refs) - 1) // 2
    sems = refs[-1]
    copies = [pltpu.make_async_copy(refs[n], refs[count + n], sems.at[n]) for n in range(count)]
    for copy in copies:
        copy.start()
    for copy in copies:
        copy.wait()


def tree(parts):
    while len(parts) > 1:
        parts = [parts[n] + parts[n + 1] for n in range(0, len(parts), 2)]
    return parts[0]


def sample_kernel(scale, *refs):
    out_ref = refs[-1]
    width = out_ref.shape[1]
    rows = -(-width // 8) * 8
    side = rows * SIDE // 128
    parts = [ref[...].astype(F32) * scale for ref in refs[:-1]]
    half = len(parts) // 2
    here = tree([part[:side] for part in parts[0::2]])
    there = tree([part[:side] for part in parts[1::2]])
    above = tree([part[side : 2 * side] for part in parts[:half]])
    below = tree([part[side : 2 * side] for part in parts[half:]])
    packed = tree([part[2 * side :] for part in parts])
    low, high = (bit == 0 for bit in sample_bits())
    quarters = (
        jnp.where(low, here, there),
        jnp.where(low, there, here),
        jnp.where(high, above, below),
        jnp.where(high, below, above),
    )
    last = [pltpu.roll(packed, (128 - r * LEFT) % 128, 1) for r in range(rows // 8)]
    total = jnp.concatenate(
        [unlisted(quarter, rows) for quarter in quarters] + [jnp.concatenate(last, axis=0)], axis=1
    )
    total = total[:width]
    for n in range(out_ref.shape[0]):
        out_ref[n] = total[:, n * CIN : (n + 1) * CIN]


def flipped(size, bits):
    return [(i, i ^ bits) for i in range(size)]


def per_device(slabs, weight, cotangent):
    samples, planes, rows, lanes = slabs.shape
    outs = planes // 2
    space = lax.axis_size("space")
    sample = lax.axis_size("sample")
    depth = space // 2
    width = COUT // space
    high = -(-width // 8) * 8
    kept_rows = depth * high
    terms = (kept_rows, TERMS)
    side = high * SIDE // 128
    part = (2 * side + 8, 128)
    cells = lanes // BLOCK
    per_out = cells * 16
    count = outs * per_out

    in_chip = flipped(space, 1)
    onward = [(i, (i + 1) % space) for i in range(space)]
    back = [(b, a) for a, b in onward]

    x = slabs.reshape(planes, rows, lanes)
    cot = cotangent.reshape(outs, rows // 2, lanes)
    w = weight.reshape(TAPS, 3 * CIN, COUT)
    vmem = pl.BlockSpec(memory_space=pltpu.VMEM)
    hbm = pl.BlockSpec(memory_space=pltpu.HBM)
    params = pltpu.CompilerParams(vmem_limit_bytes=VMEM_LIMIT)
    shape = jax.ShapeDtypeStruct
    flops = 2 * count * TAPS * SPAN * BLOCK

    edge, split, order = pl.pallas_call(
        functools.partial(edge_kernel, width),
        out_shape=(
            shape((rows, lanes), BF16),
            shape((3 * planes * 16, planes * 32), BF16),
            shape((4 * kept_rows, 2 * COUT), BF16),
        ),
        in_specs=[hbm],
        out_specs=(vmem,) * 3,
        scratch_shapes=[pltpu.SemaphoreType.DMA(())],
        compiler_params=params,
        cost_estimate=pl.CostEstimate(flops=0, bytes_accessed=10 << 20, transcendentals=0),
        name="edge_plane",
    )(pltpu.with_memory_space_constraint(x, pltpu.HBM))
    above = lax.ppermute(edge, "space", onward)
    wide, even_band, odd_band, preact, w_in = pl.pallas_call(
        own_kernel,
        out_shape=(
            shape((count, TAPS * SPAN), BF16),
            shape((TAPS * BLOCK, COUT), BF16),
            shape((TAPS * BLOCK, COUT), BF16),
            shape((count, BLOCK), F32),
            shape(w.shape, BF16),
        ),
        in_specs=[vmem, vmem, hbm],
        out_specs=(vmem,) * 5,
        scratch_shapes=[pltpu.SemaphoreType.DMA(())],
        compiler_params=params,
        cost_estimate=pl.CostEstimate(flops=flops, bytes_accessed=12 << 20, transcendentals=0),
        name="own_planes",
    )(x, split, pltpu.with_memory_space_constraint(w, pltpu.HBM))

    act, grad, first, turned, halo, send = pl.pallas_call(
        halo_kernel,
        out_shape=(
            shape(cot.shape, BF16),
            shape((count, BLOCK), BF16),
            shape((per_out, BLOCK), BF16),
            shape((4 * kept_rows, count), BF16),
            shape((per_out, 3 * SPAN), BF16),
            shape(terms, BF16),
        ),
        in_specs=[vmem] * 7,
        out_specs=(vmem,) * 6,
        scratch_shapes=[pltpu.VMEM(terms, F32)],
        compiler_params=params,
        cost_estimate=pl.CostEstimate(
            flops=flops // 2, bytes_accessed=8 << 20, transcendentals=count * BLOCK
        ),
        name="halo_and_sent_half",
    )(above, order, wide, even_band, odd_band, preact, cot)
    got = lax.ppermute(send, "space", in_chip)
    keep = pl.pallas_call(
        keep_kernel,
        out_shape=shape(terms, F32),
        in_specs=[vmem] * 3,
        out_specs=vmem,
        compiler_params=params,
        cost_estimate=pl.CostEstimate(flops=flops // 2, bytes_accessed=8 << 20, transcendentals=0),
        name="kept_half",
    )(turned, halo, wide)

    half = depth // 2
    batch = (
        shape((half,) + part, F32),
        shape((half, side, 128), BF16),
        shape((half, side, 128), BF16),
    )
    first, early_mine, early_low, early_high, later_mine, later_low, later_high = pl.pallas_call(
        pair_kernel,
        out_shape=(shape(first.shape, BF16),) + batch * 2,
        in_specs=[vmem] * 3,
        out_specs=(vmem,) * 7,
        compiler_params=params,
        name="pair_sum",
    )(keep, got, first)
    below = lax.ppermute(first, "space", back)

    def crossed(low_half, high_half):
        return (
            lax.ppermute(low_half, "sample", flipped(sample, 1)),
            lax.ppermute(high_half, "sample", flipped(sample, sample // 2)),
        )

    early = crossed(early_low, early_high)
    later = crossed(later_low, later_high)
    leaving = pl.pallas_call(
        cross_kernel,
        out_shape=(shape(part, BF16),) * half,
        in_specs=[vmem] * 3,
        out_specs=(vmem,) * half,
        compiler_params=params,
        name="early_cross_sum",
    )(early_mine, *early)
    came = [
        lax.ppermute(leaving[k - half], "space", flipped(space, 2 * k)) for k in range(half, depth)
    ]
    own, *leaving = pl.pallas_call(
        functools.partial(later_cross_kernel, half),
        out_shape=(shape(part, F32),) + (shape(part, BF16),) * (half - 1),
        in_specs=[vmem] * (half + 3),
        out_specs=(vmem,) * half,
        compiler_params=params,
        name="later_cross_sum",
    )(*leaving, later_mine, *later)
    came += [lax.ppermute(leaving[k - 1], "space", flipped(space, 2 * k)) for k in range(1, half)]

    grad_in, done = pl.pallas_call(
        input_kernel,
        out_shape=(shape(x.shape, BF16), shape((8, 128), F32)),
        in_specs=[vmem] * 3,
        out_specs=(vmem, vmem),
        scratch_shapes=[pltpu.VMEM((TAPS * SPAN, BLOCK), BF16)],
        compiler_params=params,
        cost_estimate=pl.CostEstimate(flops=flops, bytes_accessed=8 << 20, transcendentals=0),
        name="input_grad",
    )(grad, below, w_in)

    total = pl.pallas_call(
        depth_kernel,
        out_shape=shape(part, BF16),
        in_specs=[vmem] * (depth + 1),
        out_specs=vmem,
        compiler_params=params,
        name="depth_sum",
    )(done, own, *came)
    act, grad_in = pl.pallas_call(
        store_kernel,
        out_shape=(shape(cot.shape, BF16), shape(x.shape, BF16)),
        in_specs=[vmem] * 3,
        out_specs=(hbm, hbm),
        scratch_shapes=[pltpu.SemaphoreType.DMA((2,))],
        compiler_params=params,
        name="store",
    )(total, act, grad_in)
    others = [lax.ppermute(total, "sample", flipped(sample, j)) for j in range(1, sample)]
    kernel_grad = pl.pallas_call(
        functools.partial(sample_kernel, 1.0 / (samples * sample)),
        out_shape=shape((TAPS * 3, width, CIN), F32),
        in_specs=[vmem] * sample,
        out_specs=vmem,
        compiler_params=params,
        name="sample_sum",
    )(total, *others)
    kernel_grad = jnp.transpose(kernel_grad, (0, 2, 1)).reshape(3, 3, 3, CIN, width)
    return act.reshape(cotangent.shape), grad_in.reshape(slabs.shape), kernel_grad


def solution(mesh):
    placed = (P("sample", "space", None, None), P(), P("sample", "space", None, None))
    return jax.shard_map(
        per_device,
        mesh=mesh,
        in_specs=placed,
        out_specs=(
            P("sample", "space", None, None),
            P("sample", "space", None, None),
            P(None, None, None, None, "space"),
        ),
        check_vma=False,
    )
```

```python
import functools

import jax
import jax.numpy as jnp
from jax import lax
from jax.experimental import pallas as pl
from jax.experimental.pallas import tpu as pltpu
from jax.sharding import PartitionSpec as P

CIN = 96
COUT = 192
BLOCK = 384
SPAN = 512
TAPS = 9
SIDE = 640
REST = 4 * SIDE
TERMS = REST + 128
LEFT = TAPS * 3 * CIN - REST
F32 = jnp.float32
BF16 = jnp.bfloat16
VMEM_LIMIT = 12 * 1024 * 1024


def iota(shape, axis):
    return lax.broadcasted_iota(jnp.int32, shape, axis)


def row_split(planes):
    shape = (3 * planes * 16, planes * 32)
    row = iota(shape, 0)
    col = iota(shape, 1)
    j = row & 15
    plane = (row >> 4) & (planes - 1)
    b = jnp.where(row >= planes * 32, 2, jnp.where(row >= planes * 16, 1, 0))
    hit = (col == plane * 32 + 2 * j + b - 1) & ((j + b) > 0)
    return jnp.where(hit, 1.0, 0.0).astype(BF16)


def blank(rows, lanes):
    return jnp.zeros((rows, lanes), BF16)


def dot(lhs, rhs):
    return jnp.dot(lhs, rhs, preferred_element_type=F32)


def dot_nt(lhs, rhs):
    return lax.dot_general(lhs, rhs, (((1,), (1,)), ((), ())), preferred_element_type=F32)


def put(wide, per_out, cells, i, m, tap, piece):
    at = i * per_out + m * 16
    wide[at : at + 16, tap * SPAN + 128 : tap * SPAN + 512] = piece
    if m + 1 < cells:
        wide[at + 16 : at + 32, tap * SPAN : tap * SPAN + 128] = piece[:, 256:]
    if m == 0:
        wide[at : at + 16, tap * SPAN : tap * SPAN + 128] = jnp.zeros((16, 128), BF16)


def edge_kernel(x_hbm, edge_ref, split_ref, sem):
    copy = pltpu.make_async_copy(x_hbm.at[x_hbm.shape[0] - 1], edge_ref, sem)
    copy.start()
    split_ref[...] = row_split(x_hbm.shape[0])
    copy.wait()


def fill_order(order_ref, width):
    at = lax.axis_index("space")
    core = at % 2
    chip = at // 2
    steps = lax.axis_size("space") // 2
    shape = order_ref.shape
    rows = shape[0] // 4
    high = rows // steps
    inner = iota(shape, 0)
    kept = inner >= 2 * rows
    inner = inner - jnp.where(kept, 2 * rows, 0)
    odd = inner >= rows
    inner = inner - jnp.where(odd, rows, 0)
    source = jnp.where(kept, core, 1 - core) * width + jnp.where(odd, COUT, 0)
    for k in range(steps):
        channel = inner - k * high
        inside = (channel >= 0) & (channel < width)
        source = source + jnp.where(inside, channel + (chip ^ k) * 2 * width, 0)
        if high != width:
            source = jnp.where((channel >= width) & (channel < high), -1, source)
    order_ref[...] = jnp.where(iota(shape, 1) == source, 1.0, 0.0).astype(BF16)


def by_parity(wide, even_band, odd_band, taps):
    sides = []
    for start, band in ((0, even_band), (SPAN - BLOCK, odd_band)):
        windows = [wide[:, tap * SPAN + start : tap * SPAN + start + BLOCK] for tap in range(taps)]
        sides.append(dot(jnp.concatenate(windows, axis=1), band[: taps * BLOCK]))
    return sides


def own_kernel(
    width, x_ref, split_ref, w_hbm, wide, even_band, odd_band, preact, w_ref, order_ref, sem
):
    planes = x_ref.shape[0]
    outs = planes // 2
    cells = x_ref.shape[2] // BLOCK
    per_out = cells * 16
    copy = pltpu.make_async_copy(w_hbm, w_ref, sem)
    copy.start()
    fill_order(order_ref, width)
    split = split_ref[...]
    wide[0:per_out, 0 : 3 * SPAN] = jnp.zeros((per_out, 3 * SPAN), BF16)
    x = x_ref[...].reshape(planes * 32, x_ref.shape[2])
    for m in range(cells):
        rows = dot(split, x[:, m * BLOCK : (m + 1) * BLOCK]).astype(BF16)
        for b in range(3):
            for p in range(planes):
                piece = rows[(b * planes + p) * 16 : (b * planes + p + 1) * 16]
                if p % 2 == 0:
                    put(wide, per_out, cells, p // 2, m, 3 + b, piece)
                else:
                    put(wide, per_out, cells, p // 2, m, 6 + b, piece)
                    if p // 2 + 1 < outs:
                        put(wide, per_out, cells, p // 2 + 1, m, b, piece)
    copy.wait()
    for tap in range(TAPS):
        at = tap * BLOCK
        even_band[at : at + 32] = blank(32, COUT)
        even_band[at + 32 : at + 320] = w_ref[tap]
        even_band[at + 320 : at + BLOCK] = blank(64, COUT)
        odd_band[at : at + 96] = blank(96, COUT)
        odd_band[at + 96 : at + BLOCK] = w_ref[tap]
    even, odd = by_parity(wide, even_band, odd_band, TAPS)
    preact[:, :COUT] = even
    preact[:, COUT:] = odd


def add_terms(turned, edge, wide, terms):
    rows = terms.shape[0]
    per_out = edge.shape[0]
    terms[...] = jnp.zeros_like(terms)
    lane = iota((rows, SPAN), 1)
    even_lanes = (lane >= 32) & (lane < 320)
    odd_lanes = lane >= 224
    for tap in range(TAPS):
        lanes = slice(tap * SPAN, (tap + 1) * SPAN)
        if tap < 3:
            cols = jnp.concatenate([edge[:, lanes], wide[per_out:, lanes]], axis=0)
        else:
            cols = wide[:, lanes]
        both = dot(turned, cols)
        base = tap * 288 // 128 * 128
        shift = tap * 288 - base
        even = jnp.where(even_lanes, both[:rows], 0.0)
        odd = jnp.where(odd_lanes, both[rows:], 0.0)
        even = pltpu.roll(even, (shift - 32) % SPAN, 1)
        odd = pltpu.roll(odd, (shift - 224) % SPAN, 1)
        terms[:, base : base + BLOCK] += (even + odd)[:, :BLOCK]


def halo_kernel(
    above_ref, order_ref, wide, even_band, odd_band, pre_ref, cot_ref,
    act_ref, gp_ref, first_ref, turned_ref, edge, send_ref, terms,
):
    outs = cot_ref.shape[0]
    cells = cot_ref.shape[2] // BLOCK
    per_out = cells * 16
    top = lax.axis_index("space") == 0
    split_one = row_split(1)
    for m in range(cells):
        lanes = slice(m * BLOCK, (m + 1) * BLOCK)
        plane = above_ref[:, lanes]
        plane = jnp.where(top, jnp.zeros_like(plane), plane)
        above = dot(split_one, plane).astype(BF16)
        for b in range(3):
            put(edge, per_out, cells, 0, m, b, above[b * 16 : b * 16 + 16])
    added = jnp.concatenate(by_parity(edge, even_band, odd_band, 3), axis=1)
    for i in range(outs):
        for m in range(cells):
            lanes = slice(m * BLOCK, (m + 1) * BLOCK)
            at = i * per_out + m * 16
            value = pre_ref[at : at + 16]
            if i == 0:
                value = value + added[at : at + 16]
            sig = jax.nn.sigmoid(value)
            act_ref[i, :, lanes] = (value * sig).astype(BF16)
            grad = cot_ref[i, :, lanes].astype(F32) * (sig * (1.0 + value * (1.0 - sig)))
            grad = grad.astype(BF16)
            gp_ref[at : at + 16] = grad
            if i == 0:
                first_ref[at : at + 16] = grad

    turned_ref[...] = dot_nt(order_ref[...], gp_ref[...]).astype(BF16)
    add_terms(turned_ref[: 2 * send_ref.shape[0]], edge, wide, terms)
    send_ref[...] = terms[...].astype(BF16)


def keep_kernel(turned_ref, edge, wide, keep_ref):
    add_terms(turned_ref[2 * keep_ref.shape[0] :], edge, wide, keep_ref)


def input_kernel(gp_ref, below_ref, w_ref, out_ref, done_ref, band):
    done_ref[...] = jnp.zeros_like(done_ref)
    for tap in range(TAPS):
        w = w_ref[tap]
        even = jnp.concatenate([blank(32, COUT), w, blank(192, COUT)], axis=0)
        odd = jnp.concatenate([blank(224, COUT), w], axis=0)
        band[tap * SPAN : (tap + 1) * SPAN] = jnp.concatenate([even, odd], axis=1)
    per_out = below_ref.shape[0]
    cells = per_out // 16
    here = gp_ref[...]
    following = below_ref[...]
    last = lax.axis_index("space") == lax.axis_size("space") - 1
    following = jnp.where(last, jnp.zeros_like(following), following)
    there = jnp.concatenate([here[per_out:], following], axis=0)
    count = gp_ref.shape[0]
    outs = count // per_out
    shape = (128, 128)
    row = iota(shape, 0)
    below = jnp.where((iota(shape, 1) == row + 1) & ((row & 15) != 15), 1.0, 0.0).astype(BF16)

    def lowered(block):
        return jnp.concatenate(
            [dot(below, block[at : at + 128]).astype(BF16) for at in range(0, count, 128)], axis=0
        )

    here_low = lowered(here)
    there_low = lowered(there)

    def term(grad, a, b):
        tap = a * 3 + b
        return dot_nt(grad, band[tap * SPAN : (tap + 1) * SPAN])

    groups = {
        (0, 0): term(here, 1, 1),
        (0, 1): term(here, 1, 2) + term(here_low, 1, 0),
        (1, 0): term(here, 2, 1) + term(there, 0, 1),
        (1, 1): term(here, 2, 2) + term(here_low, 2, 0) + term(there, 0, 2) + term(there_low, 0, 0),
    }
    shape = (32, 32)
    row = iota(shape, 0)
    weave = jnp.where(iota(shape, 1) == (row >> 1) + (row & 1) * 16, 1.0, 0.0).astype(BF16)
    for i in range(outs):
        for m in range(cells):
            at = i * per_out + m * 16
            for pd in range(2):
                parts = []
                for ph in range(2):
                    y = groups[pd, ph]
                    body = y[at : at + 16, 128:512]
                    if m + 1 < cells:
                        body = jnp.concatenate(
                            [body[:, :256], body[:, 256:] + y[at + 16 : at + 32, :128]], axis=1
                        )
                    parts.append(body.astype(BF16))
                mixed = dot(weave, jnp.concatenate(parts, axis=0)).astype(BF16)
                out_ref[2 * i + pd, :, m * BLOCK : (m + 1) * BLOCK] = mixed


def sample_bits():
    at = lax.axis_index("sample")
    return at % 2, at // (lax.axis_size("sample") // 2)


def listed(block):
    rows, lanes = block.shape
    return jnp.concatenate(
        [block[r : r + 8, t : t + 128] for r in range(0, rows, 8) for t in range(0, lanes, 128)],
        axis=0,
    )


def unlisted(tiles, rows):
    across = tiles.shape[0] // rows
    return jnp.concatenate(
        [
            jnp.concatenate(
                [tiles[(r * across + t) * 8 : (r * across + t) * 8 + 8] for t in range(across)], axis=1
            )
            for r in range(rows // 8)
        ],
        axis=0,
    )


def pair_kernel(keep_ref, got_ref, mine_ref, low_ref, high_ref):
    low, high = sample_bits()
    steps, side = low_ref.shape[:2]
    rows = keep_ref.shape[0] // steps

    def total(start, lanes):
        lanes = pl.ds(pl.multiple_of(start, 128), lanes)
        return keep_ref[:, lanes] + got_ref[:, lanes].astype(F32)

    sent = total((1 - low) * SIDE, SIDE), total((3 - high) * SIDE, SIDE)
    kept = total(low * SIDE, SIDE), total((2 + high) * SIDE, SIDE)
    last = keep_ref[:, REST:] + got_ref[:, REST:].astype(F32)
    lane = iota((8, 128), 1)
    for k in range(steps):
        at = slice(k * rows, (k + 1) * rows)
        low_ref[k] = listed(sent[0][at]).astype(BF16)
        high_ref[k] = listed(sent[1][at]).astype(BF16)
        mine_ref[k, :side] = listed(kept[0][at])
        mine_ref[k, side : 2 * side] = listed(kept[1][at])
        packed = jnp.zeros((8, 128), F32)
        for r in range(rows // 8):
            tile = last[k * rows + r * 8 : k * rows + r * 8 + 8]
            packed = packed + pltpu.roll(jnp.where(lane < LEFT, tile, 0.0), r * LEFT, 1)
        mine_ref[k, 2 * side :] = packed


def cross_kernel(mine_ref, low_ref, high_ref, *out_refs):
    side = low_ref.shape[1]
    for k, out_ref in enumerate(out_refs):
        total = jnp.concatenate(
            [
                mine_ref[k, :side] + low_ref[k].astype(F32),
                mine_ref[k, side : 2 * side] + high_ref[k].astype(F32),
                mine_ref[k, 2 * side :],
            ],
            axis=0,
        )
        out_ref[...] = total.astype(out_ref.dtype)


def depth_kernel(done_ref, own_ref, *refs):
    del done_ref
    total = own_ref[...]
    for ref in refs[:-1]:
        total = total + ref[...].astype(F32)
    refs[-1][...] = total.astype(BF16)


def store_kernel(total_ref, *refs):
    del total_ref
    count = (len(refs) - 1) // 2
    sems = refs[-1]
    copies = [pltpu.make_async_copy(refs[n], refs[count + n], sems.at[n]) for n in range(count)]
    for copy in copies:
        copy.start()
    for copy in copies:
        copy.wait()


def tree(parts):
    while len(parts) > 1:
        parts = [parts[n] + parts[n + 1] for n in range(0, len(parts), 2)]
    return parts[0]


def sample_kernel(scale, *refs):
    out_ref = refs[-1]
    width = out_ref.shape[1]
    rows = -(-width // 8) * 8
    side = rows * SIDE // 128
    parts = [ref[...].astype(F32) * scale for ref in refs[:-1]]
    half = len(parts) // 2
    here = tree([part[:side] for part in parts[0::2]])
    there = tree([part[:side] for part in parts[1::2]])
    above = tree([part[side : 2 * side] for part in parts[:half]])
    below = tree([part[side : 2 * side] for part in parts[half:]])
    packed = tree([part[2 * side :] for part in parts])
    low, high = (bit == 0 for bit in sample_bits())
    quarters = (
        jnp.where(low, here, there),
        jnp.where(low, there, here),
        jnp.where(high, above, below),
        jnp.where(high, below, above),
    )
    last = [pltpu.roll(packed, (128 - r * LEFT) % 128, 1) for r in range(rows // 8)]
    total = jnp.concatenate(
        [unlisted(quarter, rows) for quarter in quarters] + [jnp.concatenate(last, axis=0)], axis=1
    )
    total = total[:width]
    for n in range(out_ref.shape[0]):
        out_ref[n] = total[:, n * CIN : (n + 1) * CIN]


def flipped(size, bits):
    return [(i, i ^ bits) for i in range(size)]


def per_device(slabs, weight, cotangent):
    samples, planes, rows, lanes = slabs.shape
    outs = planes // 2
    space = lax.axis_size("space")
    sample = lax.axis_size("sample")
    depth = space // 2
    width = COUT // space
    high = -(-width // 8) * 8
    kept_rows = depth * high
    terms = (kept_rows, TERMS)
    side = high * SIDE // 128
    part = (2 * side + 8, 128)
    cells = lanes // BLOCK
    per_out = cells * 16
    count = outs * per_out

    in_chip = flipped(space, 1)
    onward = [(i, (i + 1) % space) for i in range(space)]
    back = [(b, a) for a, b in onward]

    x = slabs.reshape(planes, rows, lanes)
    cot = cotangent.reshape(outs, rows // 2, lanes)
    w = weight.reshape(TAPS, 3 * CIN, COUT)
    vmem = pl.BlockSpec(memory_space=pltpu.VMEM)
    hbm = pl.BlockSpec(memory_space=pltpu.HBM)
    params = pltpu.CompilerParams(vmem_limit_bytes=VMEM_LIMIT)
    shape = jax.ShapeDtypeStruct
    flops = 2 * count * TAPS * SPAN * BLOCK

    edge, split = pl.pallas_call(
        edge_kernel,
        out_shape=(
            shape((rows, lanes), BF16),
            shape((3 * planes * 16, planes * 32), BF16),
        ),
        in_specs=[hbm],
        out_specs=(vmem,) * 2,
        scratch_shapes=[pltpu.SemaphoreType.DMA(())],
        compiler_params=params,
        cost_estimate=pl.CostEstimate(flops=0, bytes_accessed=10 << 20, transcendentals=0),
        name="edge_plane",
    )(pltpu.with_memory_space_constraint(x, pltpu.HBM))
    above = lax.ppermute(edge, "space", onward)
    wide, even_band, odd_band, preact, w_in, order = pl.pallas_call(
        functools.partial(own_kernel, width),
        out_shape=(
            shape((count, TAPS * SPAN), BF16),
            shape((TAPS * BLOCK, COUT), BF16),
            shape((TAPS * BLOCK, COUT), BF16),
            shape((count, BLOCK), F32),
            shape(w.shape, BF16),
            shape((4 * kept_rows, 2 * COUT), BF16),
        ),
        in_specs=[vmem, vmem, hbm],
        out_specs=(vmem,) * 6,
        scratch_shapes=[pltpu.SemaphoreType.DMA(())],
        compiler_params=params,
        cost_estimate=pl.CostEstimate(flops=flops, bytes_accessed=12 << 20, transcendentals=0),
        name="own_planes",
    )(x, split, pltpu.with_memory_space_constraint(w, pltpu.HBM))

    act, grad, first, turned, halo, send = pl.pallas_call(
        halo_kernel,
        out_shape=(
            shape(cot.shape, BF16),
            shape((count, BLOCK), BF16),
            shape((per_out, BLOCK), BF16),
            shape((4 * kept_rows, count), BF16),
            shape((per_out, 3 * SPAN), BF16),
            shape(terms, BF16),
        ),
        in_specs=[vmem] * 7,
        out_specs=(vmem,) * 6,
        scratch_shapes=[pltpu.VMEM(terms, F32)],
        compiler_params=params,
        cost_estimate=pl.CostEstimate(
            flops=flops // 2, bytes_accessed=8 << 20, transcendentals=count * BLOCK
        ),
        name="halo_and_sent_half",
    )(above, order, wide, even_band, odd_band, preact, cot)
    got = lax.ppermute(send, "space", in_chip)
    below = lax.ppermute(first, "space", back)
    keep = pl.pallas_call(
        keep_kernel,
        out_shape=shape(terms, F32),
        in_specs=[vmem] * 3,
        out_specs=vmem,
        compiler_params=params,
        cost_estimate=pl.CostEstimate(flops=flops // 2, bytes_accessed=8 << 20, transcendentals=0),
        name="kept_half",
    )(turned, halo, wide)

    mine, low, high_lanes = pl.pallas_call(
        pair_kernel,
        out_shape=(
            shape((depth,) + part, F32),
            shape((depth, side, 128), BF16),
            shape((depth, side, 128), BF16),
        ),
        in_specs=[vmem] * 2,
        out_specs=(vmem,) * 3,
        compiler_params=params,
        name="pair_sum",
    )(keep, got)
    low = lax.ppermute(low, "sample", flipped(sample, 1))
    high_lanes = lax.ppermute(high_lanes, "sample", flipped(sample, sample // 2))
    own, *leaving = pl.pallas_call(
        cross_kernel,
        out_shape=(shape(part, F32),) + (shape(part, BF16),) * (depth - 1),
        in_specs=[vmem] * 3,
        out_specs=(vmem,) * depth,
        compiler_params=params,
        name="cross_sum",
    )(mine, low, high_lanes)
    came = [
        lax.ppermute(leaving[k - 1], "space", flipped(space, 2 * k))
        for k in [*range(depth // 2, depth), *range(1, depth // 2)]
    ]

    grad_in, done = pl.pallas_call(
        input_kernel,
        out_shape=(shape(x.shape, BF16), shape((8, 128), F32)),
        in_specs=[vmem] * 3,
        out_specs=(vmem, vmem),
        scratch_shapes=[pltpu.VMEM((TAPS * SPAN, BLOCK), BF16)],
        compiler_params=params,
        cost_estimate=pl.CostEstimate(flops=flops, bytes_accessed=8 << 20, transcendentals=0),
        name="input_grad",
    )(grad, below, w_in)

    total = pl.pallas_call(
        depth_kernel,
        out_shape=shape(part, BF16),
        in_specs=[vmem] * (depth + 1),
        out_specs=vmem,
        compiler_params=params,
        name="depth_sum",
    )(done, own, *came)
    act, grad_in = pl.pallas_call(
        store_kernel,
        out_shape=(shape(cot.shape, BF16), shape(x.shape, BF16)),
        in_specs=[vmem] * 3,
        out_specs=(hbm, hbm),
        scratch_shapes=[pltpu.SemaphoreType.DMA((2,))],
        compiler_params=params,
        name="store",
    )(total, act, grad_in)
    others = [lax.ppermute(total, "sample", flipped(sample, j)) for j in range(1, sample)]
    kernel_grad = pl.pallas_call(
        functools.partial(sample_kernel, 1.0 / (samples * sample)),
        out_shape=shape((TAPS * 3, width, CIN), F32),
        in_specs=[vmem] * sample,
        out_specs=vmem,
        compiler_params=params,
        name="sample_sum",
    )(total, *others)
    kernel_grad = jnp.transpose(kernel_grad, (0, 2, 1)).reshape(3, 3, 3, CIN, width)
    return act.reshape(cotangent.shape), grad_in.reshape(slabs.shape), kernel_grad


def solution(mesh):
    placed = (P("sample", "space", None, None), P(), P("sample", "space", None, None))
    return jax.shard_map(
        per_device,
        mesh=mesh,
        in_specs=placed,
        out_specs=(
            P("sample", "space", None, None),
            P("sample", "space", None, None),
            P(None, None, None, None, "space"),
        ),
        check_vma=False,
    )
```
